256 devices in a mesh: cluster: 8 (over x, z_lo), sub: 32 (over y, z_hi, core).
Axes of the slice: x: 4, y: 4, z: 8 (z_hi: 4, z_lo: 2; z = z_hi * 2 + z_lo), core: 2. Of those that a mesh axis runs over, the one named last changes fastest.
Arguments:
- load_terms: float32 [256, 128, 1536], P(('cluster', 'sub')), may hold values from -60 to 60
- dual_operator: bfloat16 [256, 1536, 1536], P(('cluster', 'sub')), may hold values from -2 to 16, as said below
- dirichlet: bfloat16 [256, 1536, 1536], P(('cluster', 'sub')), may hold values from -2 to 16, as said below
- corner_coupling: bfloat16 [256, 1536, 24], P(('cluster', 'sub')), may hold values from -0.25 to 0.25
- coarse_inverse: float32 [768, 768], P(('cluster', 'sub')), may hold values from -2 to 4, as said below
- face_map: int32 [256, 6, 256], P(('cluster', 'sub')), may hold values from 0 to 255, as said below
- face_live: int32 [256, 6], P(('cluster', 'sub')), may hold values from 0 to 1, as said below
- corner_ids: int32 [256, 8], P(('cluster', 'sub')), may hold values from 0 to 255, as said below
Outputs:
- multipliers: float32 [256, 128, 1536], P(('cluster', 'sub'))
- residual: float32 [256, 128, 1536], P(('cluster', 'sub'))
The draws below stay inside these ranges and needn't reach their ends.
Inputs may be any that keep to these rules, and one draw needn't show every extreme that they name: face_map[d, f] is a permutation of the slots of a face; the maps of the two sides of a face pair are inverse to each other. `face_live`: equal on the two sides of a face pair. `corner_ids`: the eight corners of a subdomain are the lattice vertices (c + a, s + b + 4 * e) for a, b, e in 0 and 1, taken modulo 8 and 32; each vertex has one number and is shared by eight subdomains. `dual_operator`: each subdomain's matrix is symmetric and positive definite. `dirichlet`: each subdomain's matrix is symmetric and positive definite. `coarse_inverse`: symmetric and positive definite.
All inputs are finite; a program needn't handle non-finite values.
Results may differ from the reference program's by a relative error of at most 0.0099.
Values sent between devices are 32-bit elements; how exact they have to be, the bound alone decides.
A program may use at most 128 MiB of HBM per device.

```python
import math
import jax
import jax.numpy as jnp
from jax import lax

FACE = 256
ORDER = 1536
LOADS = 128
ITERS = 2
STRIDE = 4
CORNERS = 8
SLABS = 8
CYCLE = 32
SUBDOMAINS = 256
COARSE = 768


def symmetric_block(key, length, diag_low, diag_high, offdiag):
    first_key, second_key = jax.random.split(key, 2)
    normal = jax.random.normal(first_key, (length, length), jnp.float32)
    offpart = (normal + normal.T) * (offdiag / math.sqrt(2.0 * length))
    diagonal = jax.random.uniform(second_key, (length,), jnp.float32, diag_low, diag_high)
    matrix = offpart + jnp.diag(diagonal)
    return matrix


def draw_dual_operator(key, part):

    def single(position):
        return symmetric_block(jax.random.fold_in(key, position), ORDER, 2.0, 4.0, 0.7).astype(jnp.bfloat16)
    return lax.map(single, jnp.arange(SUBDOMAINS, dtype=jnp.int32))


def draw_dirichlet(key, part):
    base_key = jax.random.fold_in(key, 7)

    def single(position):
        return symmetric_block(jax.random.fold_in(base_key, position), ORDER, 1.5, 3.5, 0.6).astype(jnp.bfloat16)
    return lax.map(single, jnp.arange(SUBDOMAINS, dtype=jnp.int32))


def draw_coarse_inverse(key, part):
    return symmetric_block(jax.random.fold_in(key, 3), COARSE, 0.6, 1.6, 0.25)


def draw_load_terms(key, part):
    subkeys = jax.random.split(key, 3)
    values = jnp.clip(jax.random.normal(subkeys[0], (SUBDOMAINS, LOADS, ORDER), jnp.float32), -4.0, 4.0)
    device_scale = 0.6 + 1.2 * jnp.arange(SUBDOMAINS, dtype=jnp.float32) / (SUBDOMAINS - 1)
    column_scale = jnp.exp(jax.random.uniform(subkeys[1], (LOADS,), jnp.float32, math.log(0.3), math.log(3.0)))
    row_scale = jnp.exp(jax.random.uniform(subkeys[2], (ORDER,), jnp.float32, math.log(0.3), math.log(3.0)))
    values = values * device_scale[:, None, None] * column_scale[None, :, None] * row_scale[None, None, :]
    return jnp.clip(values, -60.0, 60.0)


def face_pairs():
    device = jnp.arange(SUBDOMAINS, dtype=jnp.int32)
    column = device // CYCLE
    within = device % CYCLE
    return jnp.stack([(column - 1) % SLABS * CYCLE + within, device, SUBDOMAINS + column * CYCLE + (within - 1) % CYCLE, SUBDOMAINS + device, 2 * SUBDOMAINS + column * CYCLE + (within - STRIDE) % CYCLE, 2 * SUBDOMAINS + device], axis=1)


def draw_face_map(key, part):
    pair_ids = face_pairs()

    def permute(pair_id):
        return jax.random.permutation(jax.random.fold_in(key, pair_id), FACE).astype(jnp.int32)
    permutations = jax.vmap(jax.vmap(permute))(pair_ids)
    inverse = jnp.argsort(permutations, axis=-1, stable=True).astype(jnp.int32)
    odd_faces = (jnp.arange(6, dtype=jnp.int32) % 2 == 1)[None, :, None]
    return jnp.where(odd_faces, permutations, inverse).astype(jnp.int32)


def draw_face_live(key, part):
    pair_ids = face_pairs()
    base_key = jax.random.fold_in(key, 11)

    def face_alive(pair_id):
        return (jax.random.randint(jax.random.fold_in(base_key, pair_id), (), 0, 4) > 0).astype(jnp.int32)
    return jax.vmap(jax.vmap(face_alive))(pair_ids)


def draw_corner_ids(key, part):
    numbering = jax.random.permutation(jax.random.fold_in(key, 5), SUBDOMAINS).astype(jnp.int32)
    device = jnp.arange(SUBDOMAINS, dtype=jnp.int32)
    column = device // CYCLE
    within = device % CYCLE
    corner = jnp.arange(8, dtype=jnp.int32)
    step_first = corner // 4
    step_second = corner // 2 % 2
    step_third = corner % 2
    vertex = (column[:, None] + step_first[None, :]) % SLABS * CYCLE + (within[:, None] + step_second[None, :] + STRIDE * step_third[None, :]) % CYCLE
    return jnp.take(numbering, vertex).astype(jnp.int32)


def steps_of(key, dims, cuts, smallest, largest):
    factor_of, own = 1.0, jax.random.fold_in(key, 6)
    for axis_at, blocks in cuts:
        heights = jnp.exp(jax.random.uniform(jax.random.fold_in(own, axis_at), (blocks,), jnp.float32, smallest / len(cuts), largest / len(cuts)))
        factor_of = factor_of * jnp.repeat(heights, dims[axis_at] // blocks).reshape([-1 if axis == axis_at else 1 for axis in range(len(dims))])
    return factor_of


def gaussian(stream_key, extent, spread, bound, cuts=(), held_as=jnp.bfloat16):
    gain = steps_of(stream_key, extent, cuts, -0.22, 0.18) if cuts else 1.0
    entries = jax.random.normal(stream_key, extent, jnp.float32) * spread * gain
    return jnp.minimum(jnp.maximum(entries, -bound), bound).astype(held_as)


def setup_inputs(seed: int = 0) -> dict:
    key_of = jax.random.split(jax.random.key(seed), 9)
    load_terms = draw_load_terms(jax.random.fold_in(key_of[8], 71), 0)
    dual_operator = draw_dual_operator(jax.random.fold_in(key_of[8], 71), 0)
    dirichlet = draw_dirichlet(jax.random.fold_in(key_of[8], 71), 0)
    corner_coupling = gaussian(key_of[3], (SUBDOMAINS, ORDER, 3 * CORNERS), (ORDER // 3) ** -0.5, 0.25, ((0, 256),))
    coarse_inverse = draw_coarse_inverse(jax.random.fold_in(key_of[8], 71), 0)
    face_map = draw_face_map(jax.random.fold_in(key_of[8], 71), 0)
    face_live = draw_face_live(jax.random.fold_in(key_of[8], 71), 0)
    corner_ids = draw_corner_ids(jax.random.fold_in(key_of[8], 71), 0)
    return dict(load_terms=load_terms, dual_operator=dual_operator, dirichlet=dirichlet, corner_coupling=corner_coupling, coarse_inverse=coarse_inverse, face_map=face_map, face_live=face_live, corner_ids=corner_ids)


def neighbour_table():
    device = jnp.arange(SUBDOMAINS, dtype=jnp.int32)
    column = device // CYCLE
    within = device % CYCLE
    return jnp.stack([((column - 1) % SLABS) * CYCLE + within, ((column + 1) % SLABS) * CYCLE + within, column * CYCLE + (within - 1) % CYCLE, column * CYCLE + (within + 1) % CYCLE, column * CYCLE + (within - STRIDE) % CYCLE, column * CYCLE + (within + STRIDE) % CYCLE], axis=1)


def assemble(field, neighbours, face_map, face_live):
    face_parts = field.reshape(SUBDOMAINS, LOADS, 6, FACE)
    pieces = []
    for face_index in range(6):
        partner = face_index ^ 1
        source = jnp.take(face_parts[:, :, partner, :], neighbours[:, face_index], axis=0)
        permuted = jnp.take_along_axis(source, face_map[:, face_index][:, None, :], axis=2)
        live_weight = face_live[:, face_index].astype(jnp.float32)[:, None, None]
        pieces.append((face_parts[:, :, face_index, :] + permuted) * live_weight)
    return jnp.stack(pieces, axis=2).reshape(SUBDOMAINS, LOADS, ORDER)


def inner_product(first_field, second_field):
    return 0.5 * jnp.sum(first_field * second_field, axis=(0, 2))


def single_product(operand_pair):
    return jnp.dot(operand_pair[0].astype(jnp.float32), operand_pair[1].astype(jnp.float32), precision=lax.Precision.HIGHEST)


def local_product(rounded, matrices):
    return lax.map(single_product, (rounded, matrices))


def reference(load_terms, dual_operator, dirichlet, corner_coupling, coarse_inverse, face_map, face_live, corner_ids):
    neighbours = neighbour_table()
    coarse_index = (3 * corner_ids[:, :, None] + jnp.arange(3, dtype=jnp.int32)[None, None, :]).reshape(SUBDOMAINS, 3 * CORNERS)
    flat_index = coarse_index.reshape(-1)
    coupling_wide = corner_coupling.astype(jnp.float32)

    def apply_dual(vector):
        rounded = lax.optimization_barrier(vector.astype(jnp.bfloat16))
        direct = local_product(rounded, dual_operator)
        corner_terms = jnp.einsum("dkm,dmc->dkc", rounded.astype(jnp.float32), coupling_wide, precision=lax.Precision.HIGHEST)
        coarse_load = jnp.zeros((LOADS, COARSE), jnp.float32).at[:, flat_index].add(jnp.transpose(corner_terms, (1, 0, 2)).reshape(LOADS, SUBDOMAINS * 3 * CORNERS))
        coarse_field = jnp.dot(coarse_load, coarse_inverse.T, precision=lax.Precision.HIGHEST)
        picked = jnp.take(coarse_field, flat_index, axis=1).reshape(LOADS, SUBDOMAINS, 3 * CORNERS)
        picked = jnp.transpose(picked, (1, 0, 2))
        corner_values = lax.optimization_barrier(picked.astype(jnp.bfloat16))
        back = jnp.einsum("dkc,dmc->dkm", corner_values.astype(jnp.float32), coupling_wide, precision=lax.Precision.HIGHEST)
        return assemble(direct + back, neighbours, face_map, face_live)

    def apply_precond(vector):
        rounded = lax.optimization_barrier(vector.astype(jnp.bfloat16))
        return assemble(local_product(rounded, dirichlet), neighbours, face_map, face_live)

    right_side = assemble(load_terms, neighbours, face_map, face_live)
    multipliers = jnp.zeros_like(right_side)
    residual = right_side
    precond = apply_precond(residual)
    residual_dot = inner_product(residual, precond)
    direction = precond
    for iteration in range(ITERS):
        dual_image = apply_dual(direction)
        step_size = residual_dot / inner_product(direction, dual_image)
        multipliers = multipliers + step_size[None, :, None] * direction
        residual = residual - step_size[None, :, None] * dual_image
        if iteration + 1 < ITERS:
            precond = apply_precond(residual)
            residual_new = inner_product(residual, precond)
            direction = precond + (residual_new / residual_dot)[None, :, None] * direction
            residual_dot = residual_new
    return multipliers, residual
```

```python
import functools

import jax
import jax.numpy as jnp
from jax import lax
from jax.experimental import pallas as pl
from jax.experimental.pallas import tpu as pltpu
from jax.sharding import PartitionSpec as P

MESH = pl.DeviceIdType.MESH
F32 = jnp.float32
BF16 = jnp.bfloat16
ROWS = 128
FACE = 256
ORDER = 1536
HALF = 384
SEND_ORDER = (4, 5, 2, 3, 0, 1)
NT = (((1,), (1,)), ((), ()))


def iota(shape, dim):
    return lax.broadcasted_iota(jnp.int32, shape, dim)


def third(value):
    return (value * 171) >> 9


def kernel(
    load_hbm,
    oper_hbm,
    prec_hbm,
    coup_ref,
    kinv_ref,
    map_ref,
    live_ref,
    ids_ref,
    mult_out,
    res_out,
    oper,
    prec,
    loads,
    resid,
    direc,
    outgo,
    income,
    permute,
    own_bt,
    wide,
    pick,
    spread,
    bmsg,
    brecv,
    kown,
    kplane,
    ksel,
    lsend,
    lrecv,
    zsend,
    zrecv,
    csend,
    crecv,
    fsend,
    frecv,
    s1send,
    s1recv,
    s2send,
    s2recv,
    load_sem,
    oper_sem,
    face_send,
    face_recv,
    b_send,
    b_recv,
    fan_send,
    fan_recv,
):
    c = lax.axis_index("cluster")
    s = lax.axis_index("sub")
    x, z_lo = c // 2, c % 2
    y, z_hi, core = s // 8, (s // 2) % 4, s % 2
    z = z_hi * 2 + z_lo
    group = x * 4 + y
    plane = group * 2 + core
    column = z * 2 + core

    def at(px, py, pz, pcore):
        return (px * 2 + pz % 2, py * 8 + (pz // 2) * 2 + pcore)

    def plane_peer(q):
        return at(q // 8, (q // 2) % 4, z, q % 2)

    def z_peer(q):
        return at(x, y, q, core)

    def column_peer(q):
        return at(x, y, q // 2, q % 2)

    def group_peer(q):
        return at(q // 4, q % 4, z, core)

    neighbours = (
        ((c + 7) % 8, s),
        ((c + 1) % 8, s),
        (c, (s + 31) % 32),
        (c, (s + 1) % 32),
        (c, (s + 28) % 32),
        (c, (s + 4) % 32),
    )

    barrier = pltpu.get_barrier_semaphore()
    for peer in neighbours:
        pl.semaphore_signal(barrier, inc=1, device_id=peer, device_id_type=MESH)

    def greet(peer_of, count, me):
        def body(k, carry):
            peer = peer_of(lax.rem(me + k, count))
            pl.semaphore_signal(barrier, inc=1, device_id=peer, device_id_type=MESH)
            return carry

        lax.fori_loop(1, count, body, 0)

    greet(plane_peer, 32, plane)
    greet(column_peer, 16, column)

    load_copies = []
    for face in range(6):
        copy = pltpu.make_async_copy(
            load_hbm.at[:, pl.ds(face * FACE, FACE)], loads.at[face], load_sem.at[face]
        )
        copy.start()
        load_copies.append(copy)
    prec_copy = pltpu.make_async_copy(prec_hbm, prec, oper_sem.at[0])
    oper_copy = pltpu.make_async_copy(oper_hbm, oper, oper_sem.at[1])
    prec_copy.start()
    oper_copy.start()

    def face_copy(turn, face):
        return pltpu.make_async_remote_copy(
            src_ref=loads.at[face] if turn == 0 else outgo.at[turn - 1, face],
            dst_ref=income.at[turn, face ^ 1],
            send_sem=face_send.at[turn, face],
            recv_sem=face_recv.at[turn, face ^ 1],
            device_id=neighbours[face],
            device_id_type=MESH,
        )

    def face_arrived(turn, face):
        face_copy(turn, face ^ 1).wait_recv()

    def fan_out(slot, peer_of, count, me, source_of, dest):
        def body(k, carry):
            q = lax.rem(me + k, count)
            pltpu.make_async_remote_copy(
                src_ref=source_of(q),
                dst_ref=dest.at[me],
                send_sem=fan_send.at[slot],
                recv_sem=fan_recv.at[slot],
                device_id=peer_of(q),
                device_id_type=MESH,
            ).start()
            return carry

        lax.fori_loop(1, count, body, 0)

    def fan_wait(sem, slot, dest):
        part = dest.at[pl.ds(0, dest.shape[0] - 1)]
        pltpu.make_async_copy(part, part, sem.at[slot]).wait()

    pl.semaphore_wait(barrier, 6 + 31 + 15)

    for face in SEND_ORDER:
        load_copies[face].wait()
        face_copy(0, face).start()

    unit = (iota((32, 24), 0) == iota((32, 24), 1)).astype(F32).astype(BF16)
    turned = lax.dot_general(unit, coup_ref[...], NT, preferred_element_type=F32)
    row = iota((32, 128), 0)
    which = third(row)
    part = row - 3 * which
    natural = jnp.full((32, 128), -1, jnp.int32)
    placed = jnp.full((32, 128), -1, jnp.int32)
    for k in range(8):
        number = jnp.full((32, 128), ids_ref[0, k], jnp.int32)
        nc, ns = number >> 5, number & 31
        nz = (((ns >> 1) & 3) << 1) + (nc & 1)
        np_ = ((nc >> 1) << 3) + ((ns >> 3) << 1) + (ns & 1)
        hit = which == k
        natural = jnp.where(hit, 3 * number + part, natural)
        placed = jnp.where(hit, nz * 128 + 3 * np_ + part, placed)
    placed_f = placed.astype(F32)
    for face in range(6):
        bmsg[face, :, :FACE] = turned[:, face * FACE : (face + 1) * FACE]
        bmsg[face, :, FACE:] = placed_f
    b_copies = []
    for face in SEND_ORDER:
        copy = pltpu.make_async_remote_copy(
            src_ref=bmsg.at[face],
            dst_ref=brecv.at[face ^ 1],
            send_sem=b_send.at[face],
            recv_sem=b_recv.at[face ^ 1],
            device_id=neighbours[face],
            device_id_type=MESH,
        )
        copy.start()
        b_copies.append(copy)
    own_bt[...] = turned.astype(BF16)

    kown[...] = jnp.zeros_like(kown)
    kown[0, 0:3, :] = kinv_ref[:, :HALF]
    kown[1, 0:3, :] = kinv_ref[:, HALF:]
    fan_out(0, plane_peer, 32, plane, lambda q: kown.at[q % 2], kplane)
    kplane[plane] = kown[core]

    lanes768 = iota((32, 768), 1)
    spread[...] = (
        (jnp.concatenate([natural] * 6, axis=1) == lanes768).astype(F32).astype(BF16)
    )

    def build_permute(face, carry):
        target = jnp.broadcast_to(map_ref[face], (FACE, FACE))
        hot = (iota((FACE, FACE), 0) == target).astype(F32)
        alive = live_ref[0, face].astype(F32)
        permute[face] = (hot * alive).astype(BF16)
        return carry

    lax.fori_loop(0, 6, build_permute, 0)

    def clear(turn):
        outgo[turn] = jnp.zeros((6, ROWS, FACE), F32)

    def permuted(turn, face):
        value = income[turn, face]
        high = value.astype(BF16)
        low = (value - high.astype(F32)).astype(BF16)
        both = jnp.dot(
            jnp.concatenate([high, low], axis=0), permute[face], preferred_element_type=F32
        )
        return both[:ROWS] + both[ROWS:]

    def alive_of(face):
        return live_ref[0, face].astype(F32)

    def fold(value):
        return value[:, :128] + value[:, 128:]

    def multiply(turn, face, rounded, matrix, field):
        if face < 5:
            product = jnp.dot(rounded, matrix[face], preferred_element_type=F32)
            for n in range(6):
                outgo[turn, n] += product[:, n * FACE : (n + 1) * FACE]
            return None
        total = jnp.zeros((ROWS, 128), F32)
        for n in SEND_ORDER:
            value = outgo[turn, n] + jnp.dot(
                rounded, matrix[face, :, n * FACE : (n + 1) * FACE], preferred_element_type=F32
            )
            outgo[turn, n] = value
            face_copy(turn + 1, n).start()
            total = total + fold(field[n] * value)
        return total

    def lane_row(total):
        return jnp.sum(total.T, axis=0, keepdims=True)

    def spread_rows(line):
        wide_ = jnp.broadcast_to(line, (128, 128)).T
        return jnp.concatenate([wide_, wide_], axis=1)

    def scalars_start(turn, first, second):
        s1send[turn] = jnp.concatenate([first, second, jnp.zeros((6, 128), F32)], axis=0)
        fan_out(1 + turn, group_peer, 16, group, lambda q: s1send.at[turn], s1recv.at[turn])
        s1recv[turn, group] = s1send[turn]

    def scalars_middle(turn):
        fan_wait(fan_recv, 1 + turn, s1recv.at[turn])
        s2send[turn] = jnp.sum(s1recv[turn], axis=0)
        fan_out(4 + turn, column_peer, 16, column, lambda q: s2send.at[turn], s2recv.at[turn])
        s2recv[turn, column] = s2send[turn]

    def scalars_end(turn):
        fan_wait(fan_recv, 4 + turn, s2recv.at[turn])
        return jnp.sum(s2recv[turn], axis=0)

    def coarse_start(turn, terms):
        high = terms.astype(BF16)
        rest = terms - high.astype(F32)
        middle = rest.astype(BF16)
        low = (rest - middle.astype(F32)).astype(BF16)
        stacked = jnp.concatenate([high, middle, low], axis=0)
        full = jnp.dot(stacked, spread[...], preferred_element_type=F32)
        full = full[:ROWS] + full[ROWS : 2 * ROWS] + full[2 * ROWS :]
        for half in range(2):
            lsend[turn, half] = full[:, half * HALF : (half + 1) * HALF].reshape(16, 8, HALF)
        fan_out(
            7 + turn,
            plane_peer,
            32,
            plane,
            lambda q: lsend.at[turn, q % 2, q // 2],
            lrecv.at[turn],
        )
        lrecv[turn, plane] = lsend[turn, core, group]

    def coarse_sum(turn):
        fan_wait(fan_recv, 7 + turn, lrecv.at[turn])
        zsend[turn] = jnp.sum(lrecv[turn], axis=0)
        fan_out(9 + turn, z_peer, 8, z, lambda q: zsend.at[turn], zrecv.at[turn])
        zrecv[turn, z] = zsend[turn]

    def coarse_apply(turn):
        fan_wait(fan_recv, 9 + turn, zrecv.at[turn])
        load = jnp.sum(zrecv[turn], axis=0)
        csend[turn] = lax.dot_general(
            load,
            ksel[...],
            NT,
            precision=lax.Precision.HIGHEST,
            preferred_element_type=F32,
        )
        fan_out(11 + turn, column_peer, 16, column, lambda q: csend.at[turn], crecv.at[turn])
        crecv[turn, column] = csend[turn]

    def coarse_share(turn):
        fan_wait(fan_recv, 11 + turn, crecv.at[turn])
        energy = jnp.zeros((8, 128), F32)
        pieces = []
        for plane_z in range(8):
            both = crecv[turn, 2 * plane_z] + crecv[turn, 2 * plane_z + 1]
            pieces.append(both[:, :128])
            energy = energy + both[:, :128] * both[:, 128:]
        energy = jnp.sum(energy, axis=1, keepdims=True)
        pieces[0] = jnp.where(iota((8, 128), 1) == 96, energy, pieces[0])
        fsend[turn] = jnp.concatenate(pieces, axis=1)
        fan_out(13 + turn, group_peer, 16, group, lambda q: fsend.at[turn], frecv.at[turn])
        frecv[turn, group] = fsend[turn]

    def coarse_values(turn):
        fan_wait(fan_recv, 13 + turn, frecv.at[turn])
        field = frecv[turn].reshape(ROWS, 1024)
        values = lax.dot_general(
            field.astype(BF16), pick[...], NT, preferred_element_type=F32
        ).astype(BF16)
        energy = jnp.broadcast_to(field[:, 96:97], (ROWS, FACE))
        return values, energy

    clear(0)
    prec_copy.wait()
    for face in range(6):
        face_arrived(0, face)
        value = alive_of(face) * loads[face] + permuted(0, face)
        resid[face] = value
        dots = multiply(0, face, value.astype(BF16), prec, resid)
    first_rz = lane_row(dots)

    clear(1)
    wide[...] = jnp.zeros_like(wide)
    for face in range(6):
        wide[0:32, face * FACE : (face + 1) * FACE] = (
            bmsg[face, :, :FACE] * alive_of(face)
        ).astype(BF16)
    lane = iota((32, 1024), 1).astype(F32)
    pick[...] = jnp.zeros_like(pick)
    pick[0:32, :] = (
        (jnp.concatenate([placed_f] * 8, axis=1) == lane).astype(F32).astype(BF16)
    )
    for face in range(6):
        b_copies[SEND_ORDER.index(face ^ 1)].wait_recv()
        start = 32 * (face + 1)
        wide[start : start + 32, face * FACE : (face + 1) * FACE] = jnp.dot(
            brecv[face, :, :FACE].astype(BF16), permute[face], preferred_element_type=F32
        ).astype(BF16)
        place = brecv[face, :, FACE:]
        pick[start : start + 32, :] = (
            (jnp.concatenate([place] * 8, axis=1) == lane).astype(F32).astype(BF16)
        )
    fan_wait(fan_recv, 0, kplane)
    line = iota((128, 256), 0)
    packed = third(line)
    choose = jnp.where(
        line < 96, (iota((128, 256), 1) == packed * 8 + line - 3 * packed).astype(F32), 0.0
    )
    ksel[0:128, :] = jnp.dot(
        choose,
        kplane[...].reshape(256, HALF),
        precision=lax.Precision.HIGHEST,
        preferred_element_type=F32,
    )
    line = iota((128, HALF), 0)
    packed = third(line)
    owner = (
        ((packed >> 3) * 2 + z_lo) * 32 + ((packed >> 1) & 3) * 8 + z_hi * 2 + (packed & 1)
    )
    wanted = 3 * owner + line - 3 * packed
    ksel[128:256, :] = jnp.where(
        line < 96, (iota((128, HALF), 1) + HALF * core == wanted).astype(F32), 0.0
    )

    oper_copy.wait()
    rz = None
    for iteration in range(2):
        back = 2 * iteration + 1
        terms = jnp.zeros((ROWS, 32), F32)
        for face in range(6):
            face_arrived(back, face)
            value = alive_of(face) * outgo[back - 1, face] + permuted(back, face)
            if iteration == 1:
                if face == 0:
                    scalars_middle(1)
                    new_rz = scalars_end(1)[0:1]
                    beta = spread_rows(new_rz / rz)
                    rz = new_rz
                value = value + beta * direc[face]
            direc[face] = value
            rounded = value.astype(BF16)
            terms = terms + lax.dot_general(
                rounded,
                own_bt[:, face * FACE : (face + 1) * FACE],
                NT,
                preferred_element_type=F32,
            )
            dots = multiply(back, face, rounded, oper, direc)
        coarse_start(iteration, terms)
        scalars_start(2 * iteration, lane_row(dots), first_rz)
        coarse_sum(iteration)
        scalars_middle(2 * iteration)
        coarse_apply(iteration)
        totals = scalars_end(2 * iteration)
        if iteration == 0:
            rz = totals[1:2]
            clear(2)
        coarse_share(iteration)
        if iteration == 0:
            clear(3)
        values, energy = coarse_values(iteration)
        curvature = spread_rows(totals[0:1]) + energy
        step = spread_rows(rz) / curvature
        for face in range(6):
            face_arrived(back + 1, face)
            cols = slice(face * FACE, (face + 1) * FACE)
            image = (
                alive_of(face) * outgo[back, face]
                + permuted(back + 1, face)
                + jnp.dot(values, wide[:, cols], preferred_element_type=F32)
            )
            gain = step * direc[face]
            value = resid[face] - step * image
            if iteration == 0:
                mult_out[:, cols] = gain
                resid[face] = value
                dots = multiply(2, face, value.astype(BF16), prec, resid)
            else:
                mult_out[:, cols] += gain
                res_out[:, cols] = value
        if iteration == 0:
            scalars_start(1, lane_row(dots), first_rz)

    for turn in range(5):
        for face in range(6):
            face_copy(turn, face).wait_send()
    for copy in b_copies:
        copy.wait_send()
    fan_wait(fan_send, 0, kplane)
    for turn in range(3):
        fan_wait(fan_send, 1 + turn, s1recv.at[turn])
        fan_wait(fan_send, 4 + turn, s2recv.at[turn])
    for turn in range(2):
        fan_wait(fan_send, 7 + turn, lrecv.at[turn])
        fan_wait(fan_send, 9 + turn, zrecv.at[turn])
        fan_wait(fan_send, 11 + turn, crecv.at[turn])
        fan_wait(fan_send, 13 + turn, frecv.at[turn])


def local(load_terms, oper, prec, coupling, kinv, face_map, face_live, ids):
    any_ = pl.BlockSpec(memory_space=pl.ANY)
    vmem = pl.BlockSpec(memory_space=pltpu.VMEM)
    smem = pl.BlockSpec(memory_space=pltpu.SMEM)
    dma = pltpu.SemaphoreType.DMA

    def buf(*shape, dtype=F32):
        return pltpu.VMEM(shape, dtype)

    field = jax.ShapeDtypeStruct((ROWS, ORDER), F32)
    mult, res = pl.pallas_call(
        kernel,
        out_shape=(field, field),
        in_specs=[any_, any_, any_, vmem, vmem, vmem, smem, smem],
        out_specs=(vmem, vmem),
        scratch_shapes=[
            buf(6, FACE, ORDER, dtype=BF16),
            buf(6, FACE, ORDER, dtype=BF16),
            buf(6, ROWS, FACE),
            buf(6, ROWS, FACE),
            buf(6, ROWS, FACE),
            buf(4, 6, ROWS, FACE),
            buf(5, 6, ROWS, FACE),
            buf(6, FACE, FACE, dtype=BF16),
            buf(32, ORDER, dtype=BF16),
            buf(256, ORDER, dtype=BF16),
            buf(256, 1024, dtype=BF16),
            buf(32, 768, dtype=BF16),
            buf(6, 32, 384),
            buf(6, 32, 384),
            buf(2, 8, HALF),
            buf(32, 8, HALF),
            buf(256, HALF),
            buf(2, 2, 16, 8, HALF),
            buf(2, 32, 8, HALF),
            buf(2, 8, HALF),
            buf(2, 8, 8, HALF),
            buf(2, 8, 256),
            buf(2, 16, 8, 256),
            buf(2, 8, 1024),
            buf(2, 16, 8, 1024),
            buf(3, 8, 128),
            buf(3, 16, 8, 128),
            buf(3, 8, 128),
            buf(3, 16, 8, 128),
            dma((6,)),
            dma((2,)),
            dma((5, 6)),
            dma((5, 6)),
            dma((6,)),
            dma((6,)),
            dma((15,)),
            dma((15,)),
        ],
        compiler_params=pltpu.CompilerParams(
            collective_id=0, has_side_effects=True, vmem_limit_bytes=60 * 1024 * 1024
        ),
        cost_estimate=pl.CostEstimate(
            flops=2_600_000_000, bytes_accessed=12_000_000, transcendentals=0
        ),
        name="feti_solve",
    )(
        load_terms[0],
        oper.reshape(6, FACE, ORDER),
        prec.reshape(6, FACE, ORDER),
        coupling[0],
        kinv,
        face_map.reshape(6, 1, FACE),
        face_live,
        ids,
    )
    return mult[None], res[None]


def solution(mesh):
    both = ("cluster", "sub")
    wide = P(both, None, None)
    flat = P(both, None)
    return jax.shard_map(
        local,
        mesh=mesh,
        in_specs=(wide, wide, wide, wide, flat, wide, flat, flat),
        out_specs=(wide, wide),
        check_vma=False,
    )
```

```python
import functools

import jax
import jax.numpy as jnp
from jax import lax
from jax.experimental import pallas as pl
from jax.experimental.pallas import tpu as pltpu
from jax.sharding import PartitionSpec as P

MESH = pl.DeviceIdType.MESH
F32 = jnp.float32
BF16 = jnp.bfloat16
ROWS = 128
FACE = 256
ORDER = 1536
HALF = 384
PART = 64
SEND_ORDER = (4, 5, 2, 3, 0, 1)
NT = (((1,), (1,)), ((), ()))


def iota(shape, dim):
    return lax.broadcasted_iota(jnp.int32, shape, dim)


def third(value):
    return (value * 171) >> 9


def kernel(
    load_hbm,
    oper_hbm,
    prec_hbm,
    coup_ref,
    kinv_ref,
    map_ref,
    live_ref,
    ids_ref,
    mult_out,
    res_out,
    oper,
    prec,
    loads,
    resid,
    direc,
    outgo,
    income,
    permute,
    wide,
    pick,
    spread,
    values,
    bmsg,
    brecv,
    kown,
    kplane,
    ksel,
    csave,
    dots,
    beta_rows,
    lsend,
    lrecv,
    zsend,
    zrecv,
    csend,
    crecv,
    fsend,
    frecv,
    s1send,
    s1recv,
    s2send,
    s2recv,
    load_sem,
    oper_sem,
    face_send,
    face_recv,
    b_send,
    b_recv,
    fan_send,
    fan_recv,
):
    c = lax.axis_index("cluster")
    s = lax.axis_index("sub")
    x, z_lo = c // 2, c % 2
    y, z_hi, core = s // 8, (s // 2) % 4, s % 2
    z = z_hi * 2 + z_lo
    group = x * 4 + y
    plane = group * 2 + core
    column = z * 2 + core

    def at(px, py, pz, pcore):
        return (px * 2 + pz % 2, py * 8 + (pz // 2) * 2 + pcore)

    def plane_peer(q):
        return at(q // 8, (q // 2) % 4, z, q % 2)

    def z_peer(q):
        return at(x, y, q, core)

    def column_peer(q):
        return at(x, y, q // 2, q % 2)

    def group_peer(q):
        return at(q // 4, q % 4, z, core)

    neighbours = (
        ((c + 7) % 8, s),
        ((c + 1) % 8, s),
        (c, (s + 31) % 32),
        (c, (s + 1) % 32),
        (c, (s + 28) % 32),
        (c, (s + 4) % 32),
    )

    barrier = pltpu.get_barrier_semaphore()
    for peer in neighbours:
        pl.semaphore_signal(barrier, inc=1, device_id=peer, device_id_type=MESH)

    def greet(peer_of, count, me):
        def body(k, carry):
            peer = peer_of(lax.rem(me + k, count))
            pl.semaphore_signal(barrier, inc=1, device_id=peer, device_id_type=MESH)
            return carry

        lax.fori_loop(1, count, body, 0)

    greet(plane_peer, 32, plane)
    greet(column_peer, 16, column)

    load_copies = []
    for face in range(6):
        copy = pltpu.make_async_copy(
            load_hbm.at[:, pl.ds(face * FACE, FACE)], loads.at[face], load_sem.at[face]
        )
        copy.start()
        load_copies.append(copy)
    prec_copy = pltpu.make_async_copy(prec_hbm, prec, oper_sem.at[0])
    oper_copy = pltpu.make_async_copy(oper_hbm, oper, oper_sem.at[1])
    prec_copy.start()
    oper_copy.start()

    def rows_of(half):
        return pl.ds(pl.multiple_of(half * PART, PART), PART)

    def face_copy(turn, half, face):
        rows = rows_of(half)
        return pltpu.make_async_remote_copy(
            src_ref=loads.at[face, rows] if turn == 0 else outgo.at[turn - 1, face, rows],
            dst_ref=income.at[turn, face ^ 1, rows],
            send_sem=face_send.at[turn, half, face],
            recv_sem=face_recv.at[turn, half, face ^ 1],
            device_id=neighbours[face],
            device_id_type=MESH,
        )

    def face_wait(sem, turn, half, face):
        part = income.at[turn, face, rows_of(half)]
        pltpu.make_async_copy(part, part, sem.at[turn, half, face]).wait()

    def fan_out(slot, peer_of, count, me, source_of, dest):
        def body(k, carry):
            q = lax.rem(me + k, count)
            pltpu.make_async_remote_copy(
                src_ref=source_of(q),
                dst_ref=dest.at[me],
                send_sem=fan_send.at[slot],
                recv_sem=fan_recv.at[slot],
                device_id=peer_of(q),
                device_id_type=MESH,
            ).start()
            return carry

        lax.fori_loop(1, count, body, 0)

    def fan_wait(sem, slot, dest):
        part = dest.at[pl.ds(0, dest.shape[0] - 1)]
        pltpu.make_async_copy(part, part, sem.at[slot]).wait()

    pl.semaphore_wait(barrier, 6 + 31 + 15)

    for half in range(2):
        for face in SEND_ORDER:
            if half == 0:
                load_copies[face].wait()
            face_copy(0, half, face).start()

    turned = coup_ref[...].astype(F32)
    zero = jnp.zeros((8, FACE), F32)
    corner = iota((8, 128), 0)
    natural = jnp.zeros((8, 128), jnp.int32)
    placed = jnp.zeros((8, 128), jnp.int32)
    for k in range(8):
        number = jnp.full((8, 128), ids_ref[0, k], jnp.int32)
        nc, ns = number >> 5, number & 31
        nz = (((ns >> 1) & 3) << 1) + (nc & 1)
        np_ = ((nc >> 1) << 3) + ((ns >> 3) << 1) + (ns & 1)
        natural = jnp.where(corner == k, 3 * number, natural)
        placed = jnp.where(corner == k, nz * 128 + 3 * np_, placed)
    places = jnp.concatenate([natural, placed], axis=1).astype(F32)
    for face in range(6):
        bmsg[face, 0:24, :] = turned[:, face * FACE : (face + 1) * FACE]
        bmsg[face, 24:32, :] = places
    b_copies = []
    for face in SEND_ORDER:
        copy = pltpu.make_async_remote_copy(
            src_ref=bmsg.at[face],
            dst_ref=brecv.at[face ^ 1],
            send_sem=b_send.at[face],
            recv_sem=b_recv.at[face ^ 1],
            device_id=neighbours[face],
            device_id_type=MESH,
        )
        copy.start()
        b_copies.append(copy)

    kown[...] = jnp.zeros_like(kown)
    kown[0, 0:3, :] = kinv_ref[:, :HALF]
    kown[1, 0:3, :] = kinv_ref[:, HALF:]
    fan_out(0, plane_peer, 32, plane, lambda q: kown.at[q % 2], kplane)
    kplane[plane] = kown[core]

    def alive_of(face):
        return live_ref[0, face].astype(F32)

    def build_permute(face, carry):
        target = jnp.broadcast_to(map_ref[face], (FACE, FACE))
        hot = (iota((FACE, FACE), 0) == target).astype(F32)
        permute[face] = (hot * alive_of(face)).astype(BF16)
        return carry

    lax.fori_loop(0, 6, build_permute, 0)

    def clear(turn):
        def body(face, carry):
            outgo[turn, face] = jnp.zeros((ROWS, FACE), F32)
            return carry

        lax.fori_loop(0, 6, body, 0)

    row = iota((32, 128), 0)
    which = third(row)
    part = (row - 3 * which).astype(F32)

    def one_hot(message):
        first = jnp.full((32, 128), -4.0, F32)
        second = jnp.full((32, 128), -4.0, F32)
        for k in range(8):
            line = message[24 + k : 25 + k, :]
            first = jnp.where(which == k, line[:, :128] + part, first)
            second = jnp.where(which == k, line[:, 128:] + part, second)
        load = jnp.concatenate([first] * 6, axis=1) == iota((32, 768), 1).astype(F32)
        field = jnp.concatenate([second] * 8, axis=1) == iota((32, 1024), 1).astype(F32)
        return load.astype(F32).astype(BF16), field.astype(F32).astype(BF16)

    def split(value):
        high = value.astype(BF16)
        low = (value - high.astype(F32)).astype(BF16)
        return jnp.concatenate([high, low], axis=0)

    def permuted(turn, face, rows):
        both = jnp.dot(
            split(income[turn, face, rows, :]), permute[face], preferred_element_type=F32
        )
        return both[:PART] + both[PART:]

    def fold(value):
        return value[:, :128] + value[:, 128:]

    def sweep(turn, half, update, matrix, field):
        rows = rows_of(half)

        def body(face, carry):
            face_wait(face_recv, turn, half, face)
            value = update(face, rows)
            if matrix is not None:
                product = jnp.dot(
                    value.astype(BF16), matrix[face], preferred_element_type=F32
                )
                for n in range(6):
                    outgo[turn, n, rows, :] += product[:, n * FACE : (n + 1) * FACE]
            return carry

        if matrix is None:
            lax.fori_loop(0, 6, body, 0)
            return
        lax.fori_loop(0, 5, body, 0)
        face_wait(face_recv, turn, half, 5)
        rounded = update(5, rows).astype(BF16)
        total = jnp.zeros((PART, 128), F32)
        for n in SEND_ORDER:
            value = outgo[turn, n, rows, :] + jnp.dot(
                rounded, matrix[5, :, n * FACE : (n + 1) * FACE], preferred_element_type=F32
            )
            outgo[turn, n, rows, :] = value
            face_copy(turn + 1, half, n).start()
            total = total + fold(field[n, rows, :] * value)
        dots[rows, :] = total

    def both_halves(turn, update, matrix, field):
        def body(half, carry):
            sweep(turn, half, update, matrix, field)
            return carry

        lax.fori_loop(0, 2, body, 0)

    def lane_row():
        return jnp.sum(dots[...].T, axis=0, keepdims=True)

    def spread_rows(line):
        wide_ = jnp.broadcast_to(line, (128, 128)).T
        return jnp.concatenate([wide_, wide_], axis=1)

    def scalars_start(turn, first, second):
        s1send[turn] = jnp.concatenate([first, second, jnp.zeros((6, 128), F32)], axis=0)
        fan_out(1 + turn, group_peer, 16, group, lambda q: s1send.at[turn], s1recv.at[turn])
        s1recv[turn, group] = s1send[turn]

    def scalars_middle(turn):
        fan_wait(fan_recv, 1 + turn, s1recv.at[turn])
        s2send[turn] = jnp.sum(s1recv[turn], axis=0)
        fan_out(4 + turn, column_peer, 16, column, lambda q: s2send.at[turn], s2recv.at[turn])
        s2recv[turn, column] = s2send[turn]

    def scalars_end(turn):
        fan_wait(fan_recv, 4 + turn, s2recv.at[turn])
        return jnp.sum(s2recv[turn], axis=0)

    def coarse_start(turn, source):
        def body(face, terms):
            return terms + lax.dot_general(
                split(outgo[source, face]), wide[face], NT, preferred_element_type=F32
            )

        terms = lax.fori_loop(0, 6, body, jnp.zeros((2 * ROWS, 256), F32))
        terms = terms[:ROWS] + terms[ROWS:]
        high = terms.astype(BF16)
        rest = terms - high.astype(F32)
        stacked = jnp.concatenate([high, split(rest)], axis=0)
        for half in range(2):
            full = jnp.dot(
                stacked,
                spread[:, half * HALF : (half + 1) * HALF],
                preferred_element_type=F32,
            )
            full = full[:ROWS] + full[ROWS : 2 * ROWS] + full[2 * ROWS :]
            lsend[turn, half] = full.reshape(16, 8, HALF)
        fan_out(
            7 + turn,
            plane_peer,
            32,
            plane,
            lambda q: lsend.at[turn, q % 2, q // 2],
            lrecv.at[turn],
        )
        lrecv[turn, plane] = lsend[turn, core, group]

    def coarse_sum(turn):
        fan_wait(fan_recv, 7 + turn, lrecv.at[turn])
        zsend[turn] = jnp.sum(lrecv[turn], axis=0)
        fan_out(9 + turn, z_peer, 8, z, lambda q: zsend.at[turn], zrecv.at[turn])
        zrecv[turn, z] = zsend[turn]

    def coarse_apply(turn):
        fan_wait(fan_recv, 9 + turn, zrecv.at[turn])
        load = jnp.sum(zrecv[turn], axis=0)
        csend[turn] = lax.dot_general(
            load,
            ksel[...],
            NT,
            precision=lax.Precision.HIGHEST,
            preferred_element_type=F32,
        )
        fan_out(11 + turn, column_peer, 16, column, lambda q: csend.at[turn], crecv.at[turn])
        crecv[turn, column] = csend[turn]

    def coarse_share(turn):
        fan_wait(fan_recv, 11 + turn, crecv.at[turn])
        energy = jnp.zeros((8, 128), F32)
        pieces = []
        for plane_z in range(8):
            both = crecv[turn, 2 * plane_z] + crecv[turn, 2 * plane_z + 1]
            if turn == 0:
                csave[plane_z] = both
            else:
                mine = pl.ds(pl.multiple_of(group * 8, 8), 8)
                both = both + beta_rows[mine, :] * csave[plane_z]
            pieces.append(both[:, :128])
            energy = energy + both[:, :128] * both[:, 128:]
        energy = jnp.sum(energy, axis=1, keepdims=True)
        pieces[0] = jnp.where(iota((8, 128), 1) == 96, energy, pieces[0])
        fsend[turn] = jnp.concatenate(pieces, axis=1)
        fan_out(13 + turn, group_peer, 16, group, lambda q: fsend.at[turn], frecv.at[turn])
        frecv[turn, group] = fsend[turn]

    def coarse_values(turn):
        fan_wait(fan_recv, 13 + turn, frecv.at[turn])
        field = frecv[turn].reshape(ROWS, 1024)
        values[...] = lax.dot_general(
            field.astype(BF16), pick[...], NT, preferred_element_type=F32
        ).astype(BF16)
        return jnp.broadcast_to(field[:, 96:97], (ROWS, FACE))

    clear(0)

    def first_residual(face, rows):
        value = alive_of(face) * loads[face, rows, :] + permuted(0, face, rows)
        resid[face, rows, :] = value
        return value

    prec_copy.wait()
    both_halves(0, first_residual, prec, resid)
    first_rz = lane_row()

    clear(1)
    wide[...] = jnp.zeros_like(wide)
    spread[...] = jnp.zeros_like(spread)
    pick[...] = jnp.zeros_like(pick)
    for face in range(6):
        wide[face, 0:32, :] = jnp.where(
            iota((32, FACE), 0) < 24, bmsg[face] * alive_of(face), 0.0
        ).astype(BF16)
    spread[0:32, :], pick[0:32, :] = one_hot(bmsg[0])
    for face in range(6):
        b_copies[SEND_ORDER.index(face ^ 1)].wait_recv()
        start = 32 * (face + 1)
        rest = jnp.where(iota((32, FACE), 0) < 24, brecv[face], 0.0).astype(BF16)
        wide[face, start : start + 32, :] = jnp.dot(
            rest, permute[face], preferred_element_type=F32
        ).astype(BF16)
        spread[start : start + 32, :], pick[start : start + 32, :] = one_hot(brecv[face])

    coarse_start(0, 0)

    fan_wait(fan_recv, 0, kplane)
    line = iota((128, 256), 0)
    packed = third(line)
    choose = jnp.where(
        line < 96, (iota((128, 256), 1) == packed * 8 + line - 3 * packed).astype(F32), 0.0
    )
    ksel[0:128, :] = jnp.dot(
        choose,
        kplane[...].reshape(256, HALF),
        precision=lax.Precision.HIGHEST,
        preferred_element_type=F32,
    )
    line = iota((128, HALF), 0)
    packed = third(line)
    owner = (
        ((packed >> 3) * 2 + z_lo) * 32 + ((packed >> 1) & 3) * 8 + z_hi * 2 + (packed & 1)
    )
    wanted = 3 * owner + line - 3 * packed
    ksel[128:256, :] = jnp.where(
        line < 96, (iota((128, HALF), 1) + HALF * core == wanted).astype(F32), 0.0
    )
    oper_copy.wait()

    rz = None
    for iteration in range(2):
        back = 2 * iteration + 1
        if iteration == 0:
            coarse_sum(0)
        else:
            coarse_start(1, 2)
            scalars_middle(1)
            coarse_sum(1)
            new_rz = scalars_end(1)[0:1]
            beta_rows[...] = spread_rows(new_rz / rz)
            rz = new_rz

        def new_direction(face, rows):
            value = alive_of(face) * outgo[back - 1, face, rows, :] + permuted(back, face, rows)
            if iteration == 1:
                value = value + beta_rows[rows, :] * direc[face, rows, :]
            direc[face, rows, :] = value
            return value

        sweep(back, 0, new_direction, oper, direc)
        coarse_apply(iteration)
        sweep(back, 1, new_direction, oper, direc)
        scalars_start(2 * iteration, lane_row(), first_rz)
        coarse_share(iteration)
        scalars_middle(2 * iteration)
        if iteration == 0:
            clear(2)
            clear(3)
        energy = coarse_values(iteration)
        totals = scalars_end(2 * iteration)
        if iteration == 0:
            rz = totals[1:2]
        beta_rows[...] = spread_rows(rz) / (spread_rows(totals[0:1]) + energy)

        def new_residual(face, rows):
            cols = pl.ds(pl.multiple_of(face * FACE, FACE), FACE)
            image = (
                alive_of(face) * outgo[back, face, rows, :]
                + permuted(back + 1, face, rows)
                + jnp.dot(values[rows, :], wide[face], preferred_element_type=F32)
            )
            step = beta_rows[rows, :]
            gain = step * direc[face, rows, :]
            value = resid[face, rows, :] - step * image
            if iteration == 0:
                mult_out[rows, cols] = gain
                resid[face, rows, :] = value
            else:
                mult_out[rows, cols] += gain
                res_out[rows, cols] = value
            return value

        if iteration == 0:
            both_halves(2, new_residual, prec, resid)
            scalars_start(1, lane_row(), first_rz)
        else:
            both_halves(4, new_residual, None, None)

    def drain(index, carry):
        half, face = index // 6, lax.rem(index, 6)
        for turn in range(5):
            face_wait(face_send, turn, half, face)
        return carry

    lax.fori_loop(0, 12, drain, 0)
    for copy in b_copies:
        copy.wait_send()
    fan_wait(fan_send, 0, kplane)
    for turn in range(3):
        fan_wait(fan_send, 1 + turn, s1recv.at[turn])
        fan_wait(fan_send, 4 + turn, s2recv.at[turn])
    for turn in range(2):
        fan_wait(fan_send, 7 + turn, lrecv.at[turn])
        fan_wait(fan_send, 9 + turn, zrecv.at[turn])
        fan_wait(fan_send, 11 + turn, crecv.at[turn])
        fan_wait(fan_send, 13 + turn, frecv.at[turn])


def local(load_terms, oper, prec, coupling, kinv, face_map, face_live, ids):
    any_ = pl.BlockSpec(memory_space=pl.ANY)
    vmem = pl.BlockSpec(memory_space=pltpu.VMEM)
    smem = pl.BlockSpec(memory_space=pltpu.SMEM)
    dma = pltpu.SemaphoreType.DMA

    def buf(*shape, dtype=F32):
        return pltpu.VMEM(shape, dtype)

    field = jax.ShapeDtypeStruct((ROWS, ORDER), F32)
    mult, res = pl.pallas_call(
        kernel,
        out_shape=(field, field),
        in_specs=[any_, any_, any_, vmem, vmem, vmem, smem, smem],
        out_specs=(vmem, vmem),
        scratch_shapes=[
            buf(6, FACE, ORDER, dtype=BF16),
            buf(6, FACE, ORDER, dtype=BF16),
            buf(6, ROWS, FACE),
            buf(6, ROWS, FACE),
            buf(6, ROWS, FACE),
            buf(4, 6, ROWS, FACE),
            buf(5, 6, ROWS, FACE),
            buf(6, FACE, FACE, dtype=BF16),
            buf(6, 256, FACE, dtype=BF16),
            buf(256, 1024, dtype=BF16),
            buf(256, 768, dtype=BF16),
            buf(ROWS, 256, dtype=BF16),
            buf(6, 32, FACE),
            buf(6, 32, FACE),
            buf(2, 8, HALF),
            buf(32, 8, HALF),
            buf(256, HALF),
            buf(8, 8, 256),
            buf(ROWS, 128),
            buf(ROWS, 256),
            buf(2, 2, 16, 8, HALF),
            buf(2, 32, 8, HALF),
            buf(2, 8, HALF),
            buf(2, 8, 8, HALF),
            buf(2, 8, 256),
            buf(2, 16, 8, 256),
            buf(2, 8, 1024),
            buf(2, 16, 8, 1024),
            buf(3, 8, 128),
            buf(3, 16, 8, 128),
            buf(3, 8, 128),
            buf(3, 16, 8, 128),
            dma((6,)),
            dma((2,)),
            dma((5, 2, 6)),
            dma((5, 2, 6)),
            dma((6,)),
            dma((6,)),
            dma((15,)),
            dma((15,)),
        ],
        compiler_params=pltpu.CompilerParams(
            collective_id=0, has_side_effects=True, vmem_limit_bytes=60 * 1024 * 1024
        ),
        cost_estimate=pl.CostEstimate(
            flops=2_600_000_000, bytes_accessed=12_000_000, transcendentals=0
        ),
        name="feti_solve",
    )(
        load_terms[0],
        oper.reshape(6, FACE, ORDER),
        prec.reshape(6, FACE, ORDER),
        coupling[0].T,
        kinv,
        face_map.reshape(6, 1, FACE),
        face_live,
        ids,
    )
    return mult[None], res[None]


def solution(mesh):
    both = ("cluster", "sub")
    wide = P(both, None, None)
    flat = P(both, None)
    return jax.shard_map(
        local,
        mesh=mesh,
        in_specs=(wide, wide, wide, wide, flat, wide, flat, flat),
        out_specs=(wide, wide),
        check_vma=False,
    )
```

```python
import functools

import jax
import jax.numpy as jnp
from jax import lax
from jax.experimental import pallas as pl
from jax.experimental.pallas import tpu as pltpu
from jax.sharding import PartitionSpec as P

MESH = pl.DeviceIdType.MESH
F32 = jnp.float32
BF16 = jnp.bfloat16
ROWS = 128
FACE = 256
ORDER = 1536
HALF = 384
PART = 64
SEND_ORDER = (4, 5, 2, 3, 0, 1)
NT = (((1,), (1,)), ((), ()))


def iota(shape, dim):
    return lax.broadcasted_iota(jnp.int32, shape, dim)


def third(value):
    return (value * 171) >> 9


def kernel(
    load_hbm,
    oper_hbm,
    prec_hbm,
    coup_ref,
    kinv_ref,
    map_ref,
    live_ref,
    ids_ref,
    mult_out,
    res_out,
    oper,
    prec,
    loads,
    resid,
    direc,
    outgo,
    income,
    permute,
    wide,
    pick,
    spread,
    values,
    bmsg,
    brecv,
    kown,
    kplane,
    ksel,
    csave,
    dots,
    step_rows,
    beta_rows,
    zed,
    qdir,
    lsend,
    lrecv,
    zsend,
    zrecv,
    csend,
    crecv,
    fsend,
    frecv,
    s1send,
    s1recv,
    s2send,
    s2recv,
    load_sem,
    oper_sem,
    face_send,
    face_recv,
    b_send,
    b_recv,
    fan_send,
    fan_recv,
):
    c = lax.axis_index("cluster")
    s = lax.axis_index("sub")
    x, z_lo = c // 2, c % 2
    y, z_hi, core = s // 8, (s // 2) % 4, s % 2
    z = z_hi * 2 + z_lo
    group = x * 4 + y
    plane = group * 2 + core
    column = z * 2 + core

    def at(px, py, pz, pcore):
        return (px * 2 + pz % 2, py * 8 + (pz // 2) * 2 + pcore)

    def plane_peer(q):
        return at(q // 8, (q // 2) % 4, z, q % 2)

    def z_peer(q):
        return at(x, y, q, core)

    def column_peer(q):
        return at(x, y, q // 2, q % 2)

    def group_peer(q):
        return at(q // 4, q % 4, z, core)

    neighbours = (
        ((c + 7) % 8, s),
        ((c + 1) % 8, s),
        (c, (s + 31) % 32),
        (c, (s + 1) % 32),
        (c, (s + 28) % 32),
        (c, (s + 4) % 32),
    )

    barrier = pltpu.get_barrier_semaphore()
    for peer in neighbours:
        pl.semaphore_signal(barrier, inc=1, device_id=peer, device_id_type=MESH)

    def greet(peer_of, count, me):
        def body(k, carry):
            peer = peer_of(lax.rem(me + k, count))
            pl.semaphore_signal(barrier, inc=1, device_id=peer, device_id_type=MESH)
            return carry

        lax.fori_loop(1, count, body, 0)

    greet(plane_peer, 32, plane)
    greet(column_peer, 16, column)

    load_copies = []
    for face in range(6):
        copy = pltpu.make_async_copy(
            load_hbm.at[:, pl.ds(face * FACE, FACE)], loads.at[face], load_sem.at[face]
        )
        copy.start()
        load_copies.append(copy)
    prec_copy = pltpu.make_async_copy(prec_hbm, prec, oper_sem.at[0])
    oper_copy = pltpu.make_async_copy(oper_hbm, oper, oper_sem.at[1])
    prec_copy.start()
    oper_copy.start()

    def rows_of(half):
        return pl.ds(pl.multiple_of(half * PART, PART), PART)

    def face_copy(turn, half, face):
        rows = rows_of(half)
        return pltpu.make_async_remote_copy(
            src_ref=loads.at[face, rows] if turn == 0 else outgo.at[turn - 1, face, rows],
            dst_ref=income.at[turn, face ^ 1, rows],
            send_sem=face_send.at[turn, half, face],
            recv_sem=face_recv.at[turn, half, face ^ 1],
            device_id=neighbours[face],
            device_id_type=MESH,
        )

    def face_wait(sem, turn, half, face):
        part = income.at[turn, face, rows_of(half)]
        pltpu.make_async_copy(part, part, sem.at[turn, half, face]).wait()

    def fan_out(slot, peer_of, count, me, source_of, dest):
        def body(k, carry):
            q = lax.rem(me + k, count)
            pltpu.make_async_remote_copy(
                src_ref=source_of(q),
                dst_ref=dest.at[me],
                send_sem=fan_send.at[slot],
                recv_sem=fan_recv.at[slot],
                device_id=peer_of(q),
                device_id_type=MESH,
            ).start()
            return carry

        lax.fori_loop(1, count, body, 0)

    def fan_wait(sem, slot, dest):
        part = dest.at[pl.ds(0, dest.shape[0] - 1)]
        pltpu.make_async_copy(part, part, sem.at[slot]).wait()

    pl.semaphore_wait(barrier, 6 + 31 + 15)

    for face in SEND_ORDER:
        load_copies[face].wait()
        face_copy(0, 0, face).start()

    turned = coup_ref[...].astype(F32)
    zero = jnp.zeros((8, FACE), F32)
    corner = iota((8, 128), 0)
    natural = jnp.zeros((8, 128), jnp.int32)
    placed = jnp.zeros((8, 128), jnp.int32)
    for k in range(8):
        number = jnp.full((8, 128), ids_ref[0, k], jnp.int32)
        nc, ns = number >> 5, number & 31
        nz = (((ns >> 1) & 3) << 1) + (nc & 1)
        np_ = ((nc >> 1) << 3) + ((ns >> 3) << 1) + (ns & 1)
        natural = jnp.where(corner == k, 3 * number, natural)
        placed = jnp.where(corner == k, nz * 128 + 3 * np_, placed)
    places = jnp.concatenate([natural, placed], axis=1).astype(F32)
    for face in range(6):
        bmsg[face, 0:24, :] = turned[:, face * FACE : (face + 1) * FACE]
        bmsg[face, 24:32, :] = places
    b_copies = []
    for face in SEND_ORDER:
        copy = pltpu.make_async_remote_copy(
            src_ref=bmsg.at[face],
            dst_ref=brecv.at[face ^ 1],
            send_sem=b_send.at[face],
            recv_sem=b_recv.at[face ^ 1],
            device_id=neighbours[face],
            device_id_type=MESH,
        )
        copy.start()
        b_copies.append(copy)
    for face in SEND_ORDER:
        face_copy(0, 1, face).start()

    kown[...] = jnp.zeros_like(kown)
    kown[0, 0:3, :] = kinv_ref[:, :HALF]
    kown[1, 0:3, :] = kinv_ref[:, HALF:]
    fan_out(0, plane_peer, 32, plane, lambda q: kown.at[q % 2], kplane)
    kplane[plane] = kown[core]

    def alive_of(face):
        return live_ref[0, face].astype(F32)

    def build_permute(face, carry):
        target = jnp.broadcast_to(map_ref[face], (FACE, FACE))
        hot = (iota((FACE, FACE), 0) == target).astype(F32)
        permute[face] = (hot * alive_of(face)).astype(BF16)
        return carry

    lax.fori_loop(0, 6, build_permute, 0)

    def clear(face, carry):
        for turn in range(4):
            outgo[turn, face] = jnp.zeros((ROWS, FACE), F32)
        return carry

    lax.fori_loop(0, 6, clear, 0)

    row = iota((32, 128), 0)
    which = third(row)
    part = (row - 3 * which).astype(F32)

    def one_hot(message):
        first = jnp.full((32, 128), -4.0, F32)
        second = jnp.full((32, 128), -4.0, F32)
        for k in range(8):
            line = message[24 + k : 25 + k, :]
            first = jnp.where(which == k, line[:, :128] + part, first)
            second = jnp.where(which == k, line[:, 128:] + part, second)
        load = jnp.concatenate([first] * 6, axis=1) == iota((32, 768), 1).astype(F32)
        field = jnp.concatenate([second] * 8, axis=1) == iota((32, 1024), 1).astype(F32)
        return load.astype(F32).astype(BF16), field.astype(F32).astype(BF16)

    def split(value):
        high = value.astype(BF16)
        low = (value - high.astype(F32)).astype(BF16)
        return jnp.concatenate([high, low], axis=0)

    def permuted(turn, face, rows):
        both = jnp.dot(
            split(income[turn, face, rows, :]), permute[face], preferred_element_type=F32
        )
        return both[:PART] + both[PART:]

    def fold(value):
        return value[:, :128] + value[:, 128:]

    def sweep(turn, half, update, matrix, products):
        rows = slice(half * PART, (half + 1) * PART)

        def body(face, carry):
            face_wait(face_recv, turn, half, face)
            value = update(face, rows)
            if matrix is not None:
                product = jnp.dot(
                    value.astype(BF16), matrix[face], preferred_element_type=F32
                )
                for n in range(6):
                    outgo[turn, n, rows, :] += product[:, n * FACE : (n + 1) * FACE]
            return carry

        if matrix is None:
            lax.fori_loop(0, 6, body, 0)
            return
        lax.fori_loop(0, 5, body, 0)
        face_wait(face_recv, turn, half, 5)
        rounded = update(5, rows).astype(BF16)
        totals = [jnp.zeros((PART, 128), F32)] * len(products)
        for n in SEND_ORDER:
            value = outgo[turn, n, rows, :] + jnp.dot(
                rounded, matrix[5, :, n * FACE : (n + 1) * FACE], preferred_element_type=F32
            )
            outgo[turn, n, rows, :] = value
            face_copy(turn + 1, half, n).start()
            totals = [
                total + fold(make(n, rows, value))
                for total, (_, make) in zip(totals, products)
            ]
        for total, (place, _) in zip(totals, products):
            dots[place, rows, :] = total

    def lane_row(place):
        return jnp.sum(dots[place].T, axis=0, keepdims=True)

    def spread_rows(line):
        wide_ = jnp.broadcast_to(line, (128, 128)).T
        return jnp.concatenate([wide_, wide_], axis=1)

    def scalars_start(slot, places):
        lines = [lane_row(place) for place in places]
        lines.append(jnp.zeros((8 - len(places), 128), F32))
        s1send[slot] = jnp.concatenate(lines, axis=0)
        fan_out(1 + slot, group_peer, 16, group, lambda q: s1send.at[slot], s1recv.at[slot])
        s1recv[slot, group] = s1send[slot]

    def scalars_middle(slot):
        fan_wait(fan_recv, 1 + slot, s1recv.at[slot])
        s2send[slot] = jnp.sum(s1recv[slot], axis=0)
        fan_out(5 + slot, column_peer, 16, column, lambda q: s2send.at[slot], s2recv.at[slot])
        s2recv[slot, column] = s2send[slot]

    def scalars_end(slot):
        fan_wait(fan_recv, 5 + slot, s2recv.at[slot])
        return jnp.sum(s2recv[slot], axis=0)

    def coarse_start(turn, source):
        def body(face, terms):
            return terms + lax.dot_general(
                split(outgo[source, face]), wide[face], NT, preferred_element_type=F32
            )

        terms = lax.fori_loop(0, 6, body, jnp.zeros((2 * ROWS, 256), F32))
        terms = terms[:ROWS] + terms[ROWS:]
        high = terms.astype(BF16)
        rest = terms - high.astype(F32)
        stacked = jnp.concatenate([high, split(rest)], axis=0)
        for half in range(2):
            full = jnp.dot(
                stacked,
                spread[:, half * HALF : (half + 1) * HALF],
                preferred_element_type=F32,
            )
            full = full[:ROWS] + full[ROWS : 2 * ROWS] + full[2 * ROWS :]
            lsend[turn, half] = full.reshape(16, 8, HALF)
        fan_out(
            9 + turn,
            plane_peer,
            32,
            plane,
            lambda q: lsend.at[turn, q % 2, q // 2],
            lrecv.at[turn],
        )
        lrecv[turn, plane] = lsend[turn, core, group]

    def coarse_sum(turn):
        fan_wait(fan_recv, 9 + turn, lrecv.at[turn])
        zsend[turn] = jnp.sum(lrecv[turn], axis=0)
        fan_out(11 + turn, z_peer, 8, z, lambda q: zsend.at[turn], zrecv.at[turn])
        zrecv[turn, z] = zsend[turn]

    def coarse_apply(turn):
        fan_wait(fan_recv, 11 + turn, zrecv.at[turn])
        load = jnp.sum(zrecv[turn], axis=0)
        csend[turn] = lax.dot_general(
            load,
            ksel[...],
            NT,
            precision=lax.Precision.HIGHEST,
            preferred_element_type=F32,
        )
        fan_out(13 + turn, column_peer, 16, column, lambda q: csend.at[turn], crecv.at[turn])
        crecv[turn, column] = csend[turn]

    def coarse_share(turn):
        fan_wait(fan_recv, 13 + turn, crecv.at[turn])
        energy = jnp.zeros((8, 128), F32)
        cross = jnp.zeros((8, 128), F32)
        pieces = []
        for plane_z in range(8):
            both = crecv[turn, 2 * plane_z] + crecv[turn, 2 * plane_z + 1]
            field, load = both[:, :128], both[:, 128:]
            if turn == 0:
                csave[plane_z] = both
            else:
                saved = csave[plane_z]
                cross = cross + field * saved[:, 128:] + saved[:, :128] * load
            pieces.append(field)
            energy = energy + field * load
        lane = iota((8, 128), 1)
        energy = jnp.sum(energy, axis=1, keepdims=True)
        pieces[0] = jnp.where(lane == 96, energy, pieces[0])
        if turn == 1:
            cross = jnp.sum(cross, axis=1, keepdims=True)
            pieces[0] = jnp.where(lane == 97, cross, pieces[0])
        fsend[turn] = jnp.concatenate(pieces, axis=1)
        fan_out(15 + turn, group_peer, 16, group, lambda q: fsend.at[turn], frecv.at[turn])
        frecv[turn, group] = fsend[turn]

    def coarse_values(turn, half):
        rows = slice(half * PART, (half + 1) * PART)
        field = frecv[turn, 8 * half : 8 * half + 8].reshape(PART, 1024)
        energy = field[:, 96:97]
        if turn == 1:
            before = frecv[0, 8 * half : 8 * half + 8].reshape(PART, 1024)
            beta = beta_rows[rows, :]
            energy = energy + beta[:, 0:1] * (
                field[:, 97:98] + beta[:, 0:1] * before[:, 96:97]
            )
            field = field + jnp.concatenate([beta] * 4, axis=1) * before
        values[rows, :] = lax.dot_general(
            field.astype(BF16), pick[...], NT, preferred_element_type=F32
        ).astype(BF16)
        return jnp.broadcast_to(energy, (PART, FACE))

    def first_residual(face, rows):
        value = alive_of(face) * loads[face, rows, :] + permuted(0, face, rows)
        resid[face, rows, :] = value
        return value

    def first_direction(face, rows):
        value = alive_of(face) * outgo[0, face, rows, :] + permuted(1, face, rows)
        direc[face, rows, :] = value
        return value

    def second_residual(face, rows):
        cols = pl.ds(pl.multiple_of(face * FACE, FACE), FACE)
        direct = alive_of(face) * outgo[1, face, rows, :] + permuted(2, face, rows)
        qdir[face, rows, :] = direct
        image = direct + jnp.dot(values[rows, :], wide[face], preferred_element_type=F32)
        step = step_rows[rows, :]
        mult_out[rows, cols] = step * direc[face, rows, :]
        value = resid[face, rows, :] - step * image
        resid[face, rows, :] = value
        return value

    def second_precond(face, rows):
        value = alive_of(face) * outgo[2, face, rows, :] + permuted(3, face, rows)
        zed[face, rows, :] = value
        return value

    def last_residual(face, rows):
        cols = pl.ds(pl.multiple_of(face * FACE, FACE), FACE)
        step, beta = step_rows[rows, :], beta_rows[rows, :]
        image = (
            alive_of(face) * outgo[3, face, rows, :]
            + permuted(4, face, rows)
            + beta * qdir[face, rows, :]
            + jnp.dot(values[rows, :], wide[face], preferred_element_type=F32)
        )
        mult_out[rows, cols] += step * (zed[face, rows, :] + beta * direc[face, rows, :])
        res_out[rows, cols] = resid[face, rows, :] - step * image

    with_residual = lambda n, rows, value: resid[n, rows, :] * value
    with_direction = lambda n, rows, value: direc[n, rows, :] * value
    with_precond = lambda n, rows, value: zed[n, rows, :] * value
    crossed = (
        lambda n, rows, value: zed[n, rows, :] * outgo[1, n, rows, :]
        + direc[n, rows, :] * value
    )

    dots[...] = jnp.zeros_like(dots)
    prec_copy.wait()
    sweep(0, 0, first_residual, prec, [(0, with_residual)])

    wide[...] = jnp.zeros_like(wide)
    spread[...] = jnp.zeros_like(spread)
    pick[...] = jnp.zeros_like(pick)
    for face in range(6):
        wide[face, 0:32, :] = jnp.where(
            iota((32, FACE), 0) < 24, bmsg[face] * alive_of(face), 0.0
        ).astype(BF16)
    spread[0:32, :], pick[0:32, :] = one_hot(bmsg[0])
    for face in range(6):
        b_copies[SEND_ORDER.index(face ^ 1)].wait_recv()
        start = 32 * (face + 1)
        rest = jnp.where(iota((32, FACE), 0) < 24, brecv[face], 0.0).astype(BF16)
        wide[face, start : start + 32, :] = jnp.dot(
            rest, permute[face], preferred_element_type=F32
        ).astype(BF16)
        spread[start : start + 32, :], pick[start : start + 32, :] = one_hot(brecv[face])

    fan_wait(fan_recv, 0, kplane)
    line = iota((128, 256), 0)
    packed = third(line)
    choose = jnp.where(
        line < 96, (iota((128, 256), 1) == packed * 8 + line - 3 * packed).astype(F32), 0.0
    )
    ksel[0:128, :] = jnp.dot(
        choose,
        kplane[...].reshape(256, HALF),
        precision=lax.Precision.HIGHEST,
        preferred_element_type=F32,
    )
    line = iota((128, HALF), 0)
    packed = third(line)
    owner = (
        ((packed >> 3) * 2 + z_lo) * 32 + ((packed >> 1) & 3) * 8 + z_hi * 2 + (packed & 1)
    )
    wanted = 3 * owner + line - 3 * packed
    ksel[128:256, :] = jnp.where(
        line < 96, (iota((128, HALF), 1) + HALF * core == wanted).astype(F32), 0.0
    )
    sweep(0, 1, first_residual, prec, [(0, with_residual)])
    coarse_start(0, 0)
    oper_copy.wait()
    coarse_sum(0)
    sweep(1, 0, first_direction, oper, [(1, with_direction)])
    scalars_start(0, (0, 1))
    coarse_apply(0)
    scalars_middle(0)
    sweep(1, 1, first_direction, oper, [(1, with_direction)])
    scalars_start(1, (0, 1))
    coarse_share(0)

    saved = []
    fan_wait(fan_recv, 15, frecv.at[0])
    for half in range(2):
        rows = slice(half * PART, (half + 1) * PART)
        totals = scalars_end(half)
        saved.append(totals)
        energy = coarse_values(0, half)
        step_rows[rows, :] = spread_rows(totals[0:1])[rows] / (
            spread_rows(totals[1:2])[rows] + energy
        )
        if half == 0:
            scalars_middle(1)
        sweep(2, half, second_residual, prec, [(2, with_residual)])
    coarse_start(1, 2)
    coarse_sum(1)
    second = [(3, with_precond), (4, crossed)]
    sweep(3, 0, second_precond, oper, second)
    scalars_start(2, (2, 3, 4))
    coarse_apply(1)
    scalars_middle(2)
    sweep(3, 1, second_precond, oper, second)
    scalars_start(3, (2, 3, 4))
    coarse_share(1)

    fan_wait(fan_recv, 16, frecv.at[1])
    for half in range(2):
        rows = slice(half * PART, (half + 1) * PART)
        totals = scalars_end(2 + half)
        beta_line = totals[0:1] / saved[half][0:1]
        beta_rows[rows, :] = spread_rows(beta_line)[rows]
        curvature = totals[1:2] + beta_line * (totals[2:3] + beta_line * saved[half][1:2])
        energy = coarse_values(1, half)
        step_rows[rows, :] = spread_rows(totals[0:1])[rows] / (
            spread_rows(curvature)[rows] + energy
        )
        if half == 0:
            scalars_middle(3)
        sweep(4, half, last_residual, None, None)

    def drain(index, carry):
        half, face = index // 6, lax.rem(index, 6)
        for turn in range(5):
            face_wait(face_send, turn, half, face)
        return carry

    lax.fori_loop(0, 12, drain, 0)
    for copy in b_copies:
        copy.wait_send()
    fan_wait(fan_send, 0, kplane)
    for slot in range(4):
        fan_wait(fan_send, 1 + slot, s1recv.at[slot])
        fan_wait(fan_send, 5 + slot, s2recv.at[slot])
    for turn in range(2):
        fan_wait(fan_send, 9 + turn, lrecv.at[turn])
        fan_wait(fan_send, 11 + turn, zrecv.at[turn])
        fan_wait(fan_send, 13 + turn, crecv.at[turn])
        fan_wait(fan_send, 15 + turn, frecv.at[turn])


def local(load_terms, oper, prec, coupling, kinv, face_map, face_live, ids):
    any_ = pl.BlockSpec(memory_space=pl.ANY)
    vmem = pl.BlockSpec(memory_space=pltpu.VMEM)
    smem = pl.BlockSpec(memory_space=pltpu.SMEM)
    dma = pltpu.SemaphoreType.DMA

    def buf(*shape, dtype=F32):
        return pltpu.VMEM(shape, dtype)

    field = jax.ShapeDtypeStruct((ROWS, ORDER), F32)
    mult, res = pl.pallas_call(
        kernel,
        out_shape=(field, field),
        in_specs=[any_, any_, any_, vmem, vmem, vmem, smem, smem],
        out_specs=(vmem, vmem),
        scratch_shapes=[
            buf(6, FACE, ORDER, dtype=BF16),
            buf(6, FACE, ORDER, dtype=BF16),
            buf(6, ROWS, FACE),
            buf(6, ROWS, FACE),
            buf(6, ROWS, FACE),
            buf(4, 6, ROWS, FACE),
            buf(5, 6, ROWS, FACE),
            buf(6, FACE, FACE, dtype=BF16),
            buf(6, 256, FACE, dtype=BF16),
            buf(256, 1024, dtype=BF16),
            buf(256, 768, dtype=BF16),
            buf(ROWS, 256, dtype=BF16),
            buf(6, 32, FACE),
            buf(6, 32, FACE),
            buf(2, 8, HALF),
            buf(32, 8, HALF),
            buf(256, HALF),
            buf(8, 8, 256),
            buf(5, ROWS, 128),
            buf(ROWS, FACE),
            buf(ROWS, FACE),
            buf(6, ROWS, FACE),
            buf(6, ROWS, FACE),
            buf(2, 2, 16, 8, HALF),
            buf(2, 32, 8, HALF),
            buf(2, 8, HALF),
            buf(2, 8, 8, HALF),
            buf(2, 8, 256),
            buf(2, 16, 8, 256),
            buf(2, 8, 1024),
            buf(2, 16, 8, 1024),
            buf(4, 8, 128),
            buf(4, 16, 8, 128),
            buf(4, 8, 128),
            buf(4, 16, 8, 128),
            dma((6,)),
            dma((2,)),
            dma((5, 2, 6)),
            dma((5, 2, 6)),
            dma((6,)),
            dma((6,)),
            dma((17,)),
            dma((17,)),
        ],
        compiler_params=pltpu.CompilerParams(
            collective_id=0, has_side_effects=True, vmem_limit_bytes=60 * 1024 * 1024
        ),
        cost_estimate=pl.CostEstimate(
            flops=2_600_000_000, bytes_accessed=12_000_000, transcendentals=0
        ),
        name="feti_solve",
    )(
        load_terms[0],
        oper.reshape(6, FACE, ORDER),
        prec.reshape(6, FACE, ORDER),
        coupling[0].T,
        kinv,
        face_map.reshape(6, 1, FACE),
        face_live,
        ids,
    )
    return mult[None], res[None]


def solution(mesh):
    both = ("cluster", "sub")
    wide = P(both, None, None)
    flat = P(both, None)
    return jax.shard_map(
        local,
        mesh=mesh,
        in_specs=(wide, wide, wide, wide, flat, wide, flat, flat),
        out_specs=(wide, wide),
        check_vma=False,
    )
```

```python
import functools

import jax
import jax.numpy as jnp
from jax import lax
from jax.experimental import pallas as pl
from jax.experimental.pallas import tpu as pltpu
from jax.sharding import PartitionSpec as P

MESH = pl.DeviceIdType.MESH
F32 = jnp.float32
BF16 = jnp.bfloat16
ROWS = 128
FACE = 256
ORDER = 1536
HALF = 384
PART = 64
SEND_ORDER = (4, 5, 2, 3, 0, 1)
NT = (((1,), (1,)), ((), ()))


def iota(shape, dim):
    return lax.broadcasted_iota(jnp.int32, shape, dim)


def third(value):
    return (value * 171) >> 9


def kernel(
    load_hbm,
    oper_hbm,
    prec_hbm,
    coup_ref,
    kinv_ref,
    map_ref,
    live_ref,
    ids_ref,
    mult_out,
    res_out,
    oper,
    prec,
    loads,
    resid,
    direc,
    outgo,
    income,
    permute,
    wide,
    pick,
    spread,
    values,
    bmsg,
    brecv,
    kown,
    kplane,
    ksel,
    csave,
    dots,
    step_rows,
    beta_rows,
    zed,
    qdir,
    lsend,
    lrecv,
    zsend,
    zrecv,
    csend,
    crecv,
    fsend,
    frecv,
    s1send,
    s1recv,
    s2send,
    s2recv,
    load_sem,
    oper_sem,
    face_send,
    face_recv,
    b_send,
    b_recv,
    fan_send,
    fan_recv,
):
    c = lax.axis_index("cluster")
    s = lax.axis_index("sub")
    x, z_lo = c // 2, c % 2
    y, z_hi, core = s // 8, (s // 2) % 4, s % 2
    z = z_hi * 2 + z_lo
    group = x * 4 + y
    plane = group * 2 + core
    column = z * 2 + core
    side = x // 2

    def at(px, py, pz, pcore):
        return (px * 2 + pz % 2, py * 8 + (pz // 2) * 2 + pcore)

    def plane_peer(q):
        return at(q // 8, (q // 2) % 4, z, q % 2)

    def z_peer(q):
        return at(x, y, q, core)

    def column_peer(q):
        return at(x, y, q // 2, q % 2)

    def group_peer(q):
        return at(q // 4, q % 4, z, core)

    neighbours = (
        ((c + 7) % 8, s),
        ((c + 1) % 8, s),
        (c, (s + 31) % 32),
        (c, (s + 1) % 32),
        (c, (s + 28) % 32),
        (c, (s + 4) % 32),
    )

    barrier = pltpu.get_barrier_semaphore()
    for peer in neighbours:
        pl.semaphore_signal(barrier, inc=1, device_id=peer, device_id_type=MESH)

    def greet(peer_of, count, me):
        def body(k, carry):
            peer = peer_of(lax.rem(me + k, count))
            pl.semaphore_signal(barrier, inc=1, device_id=peer, device_id_type=MESH)
            return carry

        lax.fori_loop(1, count, body, 0)

    greet(plane_peer, 32, plane)
    greet(column_peer, 16, column)

    load_copies = []
    for face in range(6):
        copy = pltpu.make_async_copy(
            load_hbm.at[:, pl.ds(face * FACE, FACE)], loads.at[face], load_sem.at[face]
        )
        copy.start()
        load_copies.append(copy)
    prec_copy = pltpu.make_async_copy(prec_hbm, prec, oper_sem.at[0])
    oper_copy = pltpu.make_async_copy(oper_hbm, oper, oper_sem.at[1])
    prec_copy.start()
    oper_copy.start()

    def rows_of(half):
        return pl.ds(pl.multiple_of(half * PART, PART), PART)

    def face_copy(turn, half, face):
        rows = rows_of(half)
        return pltpu.make_async_remote_copy(
            src_ref=loads.at[face, rows] if turn == 0 else outgo.at[turn - 1, face, rows],
            dst_ref=income.at[turn, face ^ 1, rows],
            send_sem=face_send.at[turn, half, face],
            recv_sem=face_recv.at[turn, half, face ^ 1],
            device_id=neighbours[face],
            device_id_type=MESH,
        )

    def face_wait(sem, turn, half, face):
        part = income.at[turn, face, rows_of(half)]
        pltpu.make_async_copy(part, part, sem.at[turn, half, face]).wait()

    def fan_out(slot, peer_of, count, me, source_of, dest):
        def body(k, carry):
            q = lax.rem(me + k, count)
            pltpu.make_async_remote_copy(
                src_ref=source_of(q),
                dst_ref=dest.at[me],
                send_sem=fan_send.at[slot],
                recv_sem=fan_recv.at[slot],
                device_id=peer_of(q),
                device_id_type=MESH,
            ).start()
            return carry

        lax.fori_loop(1, count, body, 0)

    def fan_wait(sem, slot, dest):
        part = dest.at[pl.ds(0, dest.shape[0] - 1)]
        pltpu.make_async_copy(part, part, sem.at[slot]).wait()

    pl.semaphore_wait(barrier, 6 + 31 + 15)

    for face in SEND_ORDER:
        load_copies[face].wait()
        face_copy(0, 0, face).start()

    turned = coup_ref[...].astype(F32)
    zero = jnp.zeros((8, FACE), F32)
    corner = iota((8, 128), 0)
    natural = jnp.zeros((8, 128), jnp.int32)
    placed = jnp.zeros((8, 128), jnp.int32)
    for k in range(8):
        number = jnp.full((8, 128), ids_ref[0, k], jnp.int32)
        nc, ns = number >> 5, number & 31
        nz = (((ns >> 1) & 3) << 1) + (nc & 1)
        np_ = ((nc >> 1) << 3) + ((ns >> 3) << 1) + (ns & 1)
        natural = jnp.where(corner == k, 3 * number, natural)
        placed = jnp.where(corner == k, nz * 128 + 3 * np_, placed)
    places = jnp.concatenate([natural, placed], axis=1).astype(F32)
    for face in range(6):
        bmsg[face, 0:24, :] = turned[:, face * FACE : (face + 1) * FACE]
        bmsg[face, 24:32, :] = places
    b_copies = []
    for face in SEND_ORDER:
        copy = pltpu.make_async_remote_copy(
            src_ref=bmsg.at[face],
            dst_ref=brecv.at[face ^ 1],
            send_sem=b_send.at[face],
            recv_sem=b_recv.at[face ^ 1],
            device_id=neighbours[face],
            device_id_type=MESH,
        )
        copy.start()
        b_copies.append(copy)
    for face in SEND_ORDER:
        face_copy(0, 1, face).start()

    kown[...] = jnp.zeros_like(kown)
    kown[0, 0:3, :] = kinv_ref[:, :HALF]
    kown[1, 0:3, :] = kinv_ref[:, HALF:]
    fan_out(0, plane_peer, 32, plane, lambda q: kown.at[q % 2], kplane)
    kplane[plane] = kown[core]

    def alive_of(face):
        return live_ref[0, face].astype(F32)

    def build_permute(face, carry):
        target = jnp.broadcast_to(map_ref[face], (FACE, FACE))
        hot = (iota((FACE, FACE), 0) == target).astype(F32)
        permute[face] = (hot * alive_of(face)).astype(BF16)
        return carry

    lax.fori_loop(0, 6, build_permute, 0)

    def clear(face, carry):
        for turn in range(4):
            outgo[turn, face] = jnp.zeros((ROWS, FACE), F32)
        return carry

    lax.fori_loop(0, 6, clear, 0)

    row = iota((32, 128), 0)
    which = third(row)
    part = (row - 3 * which).astype(F32)

    def one_hot(message):
        first = jnp.full((32, 128), -4.0, F32)
        second = jnp.full((32, 128), -4.0, F32)
        for k in range(8):
            line = message[24 + k : 25 + k, :]
            first = jnp.where(which == k, line[:, :128] + part, first)
            second = jnp.where(which == k, line[:, 128:] + part, second)
        load = jnp.concatenate([first] * 6, axis=1) == iota((32, 768), 1).astype(F32)
        field = jnp.concatenate([second] * 8, axis=1) == iota((32, 1024), 1).astype(F32)
        return load.astype(F32).astype(BF16), field.astype(F32).astype(BF16)

    def split(value):
        high = value.astype(BF16)
        low = (value - high.astype(F32)).astype(BF16)
        return jnp.concatenate([high, low], axis=0)

    def permuted(turn, face, rows):
        both = jnp.dot(
            split(income[turn, face, rows, :]), permute[face], preferred_element_type=F32
        )
        return both[:PART] + both[PART:]

    def fold(value):
        return value[:, :128] + value[:, 128:]

    def sweep(turn, half, update, matrix, products):
        rows = slice(half * PART, (half + 1) * PART)

        def body(face, carry):
            face_wait(face_recv, turn, half, face)
            value = update(face, rows)
            if matrix is not None:
                product = jnp.dot(
                    value.astype(BF16), matrix[face], preferred_element_type=F32
                )
                for n in range(6):
                    outgo[turn, n, rows, :] += product[:, n * FACE : (n + 1) * FACE]
            return carry

        if matrix is None:
            lax.fori_loop(0, 6, body, 0)
            return
        lax.fori_loop(0, 5, body, 0)
        face_wait(face_recv, turn, half, 5)
        rounded = update(5, rows).astype(BF16)
        totals = [jnp.zeros((PART, 128), F32)] * len(products)
        for n in SEND_ORDER:
            value = outgo[turn, n, rows, :] + jnp.dot(
                rounded, matrix[5, :, n * FACE : (n + 1) * FACE], preferred_element_type=F32
            )
            outgo[turn, n, rows, :] = value
            face_copy(turn + 1, half, n).start()
            totals = [
                total + fold(make(n, rows, value))
                for total, (_, make) in zip(totals, products)
            ]
        for total, (place, _) in zip(totals, products):
            dots[place, rows, :] = total

    def lane_row(place):
        return jnp.sum(dots[place].T, axis=0, keepdims=True)

    def spread_rows(line):
        wide_ = jnp.broadcast_to(line, (128, 128)).T
        return jnp.concatenate([wide_, wide_], axis=1)

    def scalars_start(slot, places):
        lines = [lane_row(place) for place in places]
        lines.append(jnp.zeros((8 - len(places), 128), F32))
        s1send[slot] = jnp.concatenate(lines, axis=0)
        fan_out(1 + slot, group_peer, 16, group, lambda q: s1send.at[slot], s1recv.at[slot])
        s1recv[slot, group] = s1send[slot]

    def scalars_middle(slot):
        fan_wait(fan_recv, 1 + slot, s1recv.at[slot])
        s2send[slot] = jnp.sum(s1recv[slot], axis=0)
        fan_out(5 + slot, column_peer, 16, column, lambda q: s2send.at[slot], s2recv.at[slot])
        s2recv[slot, column] = s2send[slot]

    def scalars_end(slot):
        fan_wait(fan_recv, 5 + slot, s2recv.at[slot])
        return jnp.sum(s2recv[slot], axis=0)

    def on_side(half, step, turn):
        @pl.when(side == half)
        def _():
            step(turn)

    def coarse_start(turn, half, source):
        rows = slice(half * PART, (half + 1) * PART)

        def body(face, terms):
            return terms + lax.dot_general(
                split(outgo[source, face, rows, :]), wide[face], NT, preferred_element_type=F32
            )

        terms = lax.fori_loop(0, 6, body, jnp.zeros((2 * PART, 256), F32))
        terms = terms[:PART] + terms[PART:]
        high = terms.astype(BF16)
        rest = terms - high.astype(F32)
        stacked = jnp.concatenate([high, split(rest)], axis=0)
        for part in range(2):
            full = jnp.dot(
                stacked,
                spread[:, part * HALF : (part + 1) * HALF],
                preferred_element_type=F32,
            )
            full = full[:PART] + full[PART : 2 * PART] + full[2 * PART :]
            lsend[turn, part, 8 * half : 8 * half + 8] = full.reshape(8, 8, HALF)

        def send(k, carry):
            q = 16 * half + lax.rem(plane + k, 16)

            @pl.when(q != plane)
            def _():
                pltpu.make_async_remote_copy(
                    src_ref=lsend.at[turn, q % 2, q // 2],
                    dst_ref=lrecv.at[turn, plane],
                    send_sem=fan_send.at[9 + turn],
                    recv_sem=fan_recv.at[9 + turn],
                    device_id=plane_peer(q),
                    device_id_type=MESH,
                ).start()

            return carry

        lax.fori_loop(0, 16, send, 0)

        @pl.when(side == half)
        def _():
            lrecv[turn, plane] = lsend[turn, core, group]

    def coarse_sum(turn):
        fan_wait(fan_recv, 9 + turn, lrecv.at[turn])
        zsend[turn] = jnp.sum(lrecv[turn], axis=0)
        fan_out(11 + turn, z_peer, 8, z, lambda q: zsend.at[turn], zrecv.at[turn])
        zrecv[turn, z] = zsend[turn]

    def coarse_apply(turn):
        fan_wait(fan_recv, 11 + turn, zrecv.at[turn])
        load = jnp.sum(zrecv[turn], axis=0)
        csend[turn] = lax.dot_general(
            load,
            ksel[...],
            NT,
            precision=lax.Precision.HIGHEST,
            preferred_element_type=F32,
        )
        fan_out(13 + turn, column_peer, 16, column, lambda q: csend.at[turn], crecv.at[turn])
        crecv[turn, column] = csend[turn]

    def coarse_share(turn):
        fan_wait(fan_recv, 13 + turn, crecv.at[turn])
        energy = jnp.zeros((8, 128), F32)
        cross = jnp.zeros((8, 128), F32)
        pieces = []
        for plane_z in range(8):
            both = crecv[turn, 2 * plane_z] + crecv[turn, 2 * plane_z + 1]
            field, load = both[:, :128], both[:, 128:]
            if turn == 0:
                csave[plane_z] = both
            else:
                saved = csave[plane_z]
                cross = cross + field * saved[:, 128:] + saved[:, :128] * load
            pieces.append(field)
            energy = energy + field * load
        lane = iota((8, 128), 1)
        energy = jnp.sum(energy, axis=1, keepdims=True)
        pieces[0] = jnp.where(lane == 96, energy, pieces[0])
        if turn == 1:
            cross = jnp.sum(cross, axis=1, keepdims=True)
            pieces[0] = jnp.where(lane == 97, cross, pieces[0])
        fsend[turn] = jnp.concatenate(pieces, axis=1)
        frecv[turn, group] = fsend[turn]

        def send(k, carry):
            q = lax.rem(group + k, 16)
            pltpu.make_async_remote_copy(
                src_ref=fsend.at[turn],
                dst_ref=frecv.at[turn, group],
                send_sem=fan_send.at[15 + turn],
                recv_sem=fan_recv.at[15 + turn + 2 * side],
                device_id=group_peer(q),
                device_id_type=MESH,
            ).start()
            return carry

        lax.fori_loop(1, 16, send, 0)

    def coarse_arrived(turn, half):
        def wait(count):
            part = frecv.at[turn, pl.ds(8 * half, count)]
            pltpu.make_async_copy(part, part, fan_recv.at[15 + turn + 2 * half]).wait()

        @pl.when(side == half)
        def _():
            wait(7)

        @pl.when(side != half)
        def _():
            wait(8)

    def coarse_values(turn, half):
        rows = slice(half * PART, (half + 1) * PART)
        field = frecv[turn, 8 * half : 8 * half + 8].reshape(PART, 1024)
        energy = field[:, 96:97]
        if turn == 1:
            before = frecv[0, 8 * half : 8 * half + 8].reshape(PART, 1024)
            beta = beta_rows[rows, :]
            energy = energy + beta[:, 0:1] * (
                field[:, 97:98] + beta[:, 0:1] * before[:, 96:97]
            )
            field = field + jnp.concatenate([beta] * 4, axis=1) * before
        values[rows, :] = lax.dot_general(
            field.astype(BF16), pick[...], NT, preferred_element_type=F32
        ).astype(BF16)
        return jnp.broadcast_to(energy, (PART, FACE))

    def first_residual(face, rows):
        value = alive_of(face) * loads[face, rows, :] + permuted(0, face, rows)
        resid[face, rows, :] = value
        return value

    def first_direction(face, rows):
        value = alive_of(face) * outgo[0, face, rows, :] + permuted(1, face, rows)
        direc[face, rows, :] = value
        return value

    def second_residual(face, rows):
        cols = pl.ds(pl.multiple_of(face * FACE, FACE), FACE)
        direct = alive_of(face) * outgo[1, face, rows, :] + permuted(2, face, rows)
        qdir[face, rows, :] = direct
        image = direct + jnp.dot(values[rows, :], wide[face], preferred_element_type=F32)
        step = step_rows[rows, :]
        mult_out[rows, cols] = step * direc[face, rows, :]
        value = resid[face, rows, :] - step * image
        resid[face, rows, :] = value
        return value

    def second_precond(face, rows):
        value = alive_of(face) * outgo[2, face, rows, :] + permuted(3, face, rows)
        zed[face, rows, :] = value
        return value

    def last_residual(face, rows):
        cols = pl.ds(pl.multiple_of(face * FACE, FACE), FACE)
        step, beta = step_rows[rows, :], beta_rows[rows, :]
        image = (
            alive_of(face) * outgo[3, face, rows, :]
            + permuted(4, face, rows)
            + beta * qdir[face, rows, :]
            + jnp.dot(values[rows, :], wide[face], preferred_element_type=F32)
        )
        mult_out[rows, cols] += step * (zed[face, rows, :] + beta * direc[face, rows, :])
        res_out[rows, cols] = resid[face, rows, :] - step * image

    with_residual = lambda n, rows, value: resid[n, rows, :] * value
    with_direction = lambda n, rows, value: direc[n, rows, :] * value
    with_precond = lambda n, rows, value: zed[n, rows, :] * value
    crossed = (
        lambda n, rows, value: zed[n, rows, :] * outgo[1, n, rows, :]
        + direc[n, rows, :] * value
    )

    dots[...] = jnp.zeros_like(dots)
    prec_copy.wait()
    sweep(0, 0, first_residual, prec, [(0, with_residual)])

    wide[...] = jnp.zeros_like(wide)
    spread[...] = jnp.zeros_like(spread)
    pick[...] = jnp.zeros_like(pick)
    for face in range(6):
        wide[face, 0:32, :] = jnp.where(
            iota((32, FACE), 0) < 24, bmsg[face] * alive_of(face), 0.0
        ).astype(BF16)
    spread[0:32, :], pick[0:32, :] = one_hot(bmsg[0])
    for face in range(6):
        b_copies[SEND_ORDER.index(face ^ 1)].wait_recv()
        start = 32 * (face + 1)
        rest = jnp.where(iota((32, FACE), 0) < 24, brecv[face], 0.0).astype(BF16)
        wide[face, start : start + 32, :] = jnp.dot(
            rest, permute[face], preferred_element_type=F32
        ).astype(BF16)
        spread[start : start + 32, :], pick[start : start + 32, :] = one_hot(brecv[face])

    fan_wait(fan_recv, 0, kplane)
    line = iota((128, 256), 0)
    packed = third(line)
    choose = jnp.where(
        line < 96, (iota((128, 256), 1) == packed * 8 + line - 3 * packed).astype(F32), 0.0
    )
    ksel[0:128, :] = jnp.dot(
        choose,
        kplane[...].reshape(256, HALF),
        precision=lax.Precision.HIGHEST,
        preferred_element_type=F32,
    )
    line = iota((128, HALF), 0)
    packed = third(line)
    owner = (
        ((packed >> 3) * 2 + z_lo) * 32 + ((packed >> 1) & 3) * 8 + z_hi * 2 + (packed & 1)
    )
    wanted = 3 * owner + line - 3 * packed
    ksel[128:256, :] = jnp.where(
        line < 96, (iota((128, HALF), 1) + HALF * core == wanted).astype(F32), 0.0
    )
    coarse_start(0, 0, 0)
    sweep(0, 1, first_residual, prec, [(0, with_residual)])
    coarse_start(0, 1, 0)
    oper_copy.wait()
    on_side(0, coarse_sum, 0)
    on_side(0, coarse_apply, 0)
    sweep(1, 0, first_direction, oper, [(1, with_direction)])
    scalars_start(0, (0, 1))
    on_side(1, coarse_sum, 0)
    on_side(0, coarse_share, 0)
    on_side(1, coarse_apply, 0)
    scalars_middle(0)
    sweep(1, 1, first_direction, oper, [(1, with_direction)])
    scalars_start(1, (0, 1))
    on_side(1, coarse_share, 0)

    saved = []
    for half in range(2):
        rows = slice(half * PART, (half + 1) * PART)
        totals = scalars_end(half)
        saved.append(totals)
        coarse_arrived(0, half)
        energy = coarse_values(0, half)
        step_rows[rows, :] = spread_rows(totals[0:1])[rows] / (
            spread_rows(totals[1:2])[rows] + energy
        )
        if half == 0:
            scalars_middle(1)
        sweep(2, half, second_residual, prec, [(2, with_residual)])
        coarse_start(1, half, 2)
    second = [(3, with_precond), (4, crossed)]
    on_side(0, coarse_sum, 1)
    on_side(0, coarse_apply, 1)
    sweep(3, 0, second_precond, oper, second)
    scalars_start(2, (2, 3, 4))
    on_side(1, coarse_sum, 1)
    on_side(0, coarse_share, 1)
    on_side(1, coarse_apply, 1)
    scalars_middle(2)
    sweep(3, 1, second_precond, oper, second)
    scalars_start(3, (2, 3, 4))
    on_side(1, coarse_share, 1)

    for half in range(2):
        rows = slice(half * PART, (half + 1) * PART)
        totals = scalars_end(2 + half)
        beta_line = totals[0:1] / saved[half][0:1]
        beta_rows[rows, :] = spread_rows(beta_line)[rows]
        curvature = totals[1:2] + beta_line * (totals[2:3] + beta_line * saved[half][1:2])
        coarse_arrived(1, half)
        energy = coarse_values(1, half)
        step_rows[rows, :] = spread_rows(totals[0:1])[rows] / (
            spread_rows(curvature)[rows] + energy
        )
        if half == 0:
            scalars_middle(3)
        sweep(4, half, last_residual, None, None)

    def drain(index, carry):
        half, face = index // 6, lax.rem(index, 6)
        for turn in range(5):
            face_wait(face_send, turn, half, face)
        return carry

    lax.fori_loop(0, 12, drain, 0)
    for copy in b_copies:
        copy.wait_send()
    fan_wait(fan_send, 0, kplane)
    for slot in range(4):
        fan_wait(fan_send, 1 + slot, s1recv.at[slot])
        fan_wait(fan_send, 5 + slot, s2recv.at[slot])
    for turn in range(2):
        fan_wait(fan_send, 9 + turn, lrecv.at[turn])
        fan_wait(fan_send, 11 + turn, zrecv.at[turn])
        fan_wait(fan_send, 13 + turn, crecv.at[turn])
        fan_wait(fan_send, 15 + turn, frecv.at[turn])


def local(load_terms, oper, prec, coupling, kinv, face_map, face_live, ids):
    any_ = pl.BlockSpec(memory_space=pl.ANY)
    vmem = pl.BlockSpec(memory_space=pltpu.VMEM)
    smem = pl.BlockSpec(memory_space=pltpu.SMEM)
    dma = pltpu.SemaphoreType.DMA

    def buf(*shape, dtype=F32):
        return pltpu.VMEM(shape, dtype)

    field = jax.ShapeDtypeStruct((ROWS, ORDER), F32)
    mult, res = pl.pallas_call(
        kernel,
        out_shape=(field, field),
        in_specs=[any_, any_, any_, vmem, vmem, vmem, smem, smem],
        out_specs=(vmem, vmem),
        scratch_shapes=[
            buf(6, FACE, ORDER, dtype=BF16),
            buf(6, FACE, ORDER, dtype=BF16),
            buf(6, ROWS, FACE),
            buf(6, ROWS, FACE),
            buf(6, ROWS, FACE),
            buf(4, 6, ROWS, FACE),
            buf(5, 6, ROWS, FACE),
            buf(6, FACE, FACE, dtype=BF16),
            buf(6, 256, FACE, dtype=BF16),
            buf(256, 1024, dtype=BF16),
            buf(256, 768, dtype=BF16),
            buf(ROWS, 256, dtype=BF16),
            buf(6, 32, FACE),
            buf(6, 32, FACE),
            buf(2, 8, HALF),
            buf(32, 8, HALF),
            buf(256, HALF),
            buf(8, 8, 256),
            buf(5, ROWS, 128),
            buf(ROWS, FACE),
            buf(ROWS, FACE),
            buf(6, ROWS, FACE),
            buf(6, ROWS, FACE),
            buf(2, 2, 16, 8, HALF),
            buf(2, 32, 8, HALF),
            buf(2, 8, HALF),
            buf(2, 8, 8, HALF),
            buf(2, 8, 256),
            buf(2, 16, 8, 256),
            buf(2, 8, 1024),
            buf(2, 16, 8, 1024),
            buf(4, 8, 128),
            buf(4, 16, 8, 128),
            buf(4, 8, 128),
            buf(4, 16, 8, 128),
            dma((6,)),
            dma((2,)),
            dma((5, 2, 6)),
            dma((5, 2, 6)),
            dma((6,)),
            dma((6,)),
            dma((19,)),
            dma((19,)),
        ],
        compiler_params=pltpu.CompilerParams(
            collective_id=0, has_side_effects=True, vmem_limit_bytes=60 * 1024 * 1024
        ),
        cost_estimate=pl.CostEstimate(
            flops=2_600_000_000, bytes_accessed=12_000_000, transcendentals=0
        ),
        name="feti_solve",
    )(
        load_terms[0],
        oper.reshape(6, FACE, ORDER),
        prec.reshape(6, FACE, ORDER),
        coupling[0].T,
        kinv,
        face_map.reshape(6, 1, FACE),
        face_live,
        ids,
    )
    return mult[None], res[None]


def solution(mesh):
    both = ("cluster", "sub")
    wide = P(both, None, None)
    flat = P(both, None)
    return jax.shard_map(
        local,
        mesh=mesh,
        in_specs=(wide, wide, wide, wide, flat, wide, flat, flat),
        out_specs=(wide, wide),
        check_vma=False,
    )
```

```python
import functools

import jax
import jax.numpy as jnp
from jax import lax
from jax.experimental import pallas as pl
from jax.experimental.pallas import tpu as pltpu
from jax.sharding import PartitionSpec as P

MESH = pl.DeviceIdType.MESH
F32 = jnp.float32
BF16 = jnp.bfloat16
ROWS = 128
FACE = 256
ORDER = 1536
HALF = 384
PART = 64
SEND_ORDER = (4, 5, 2, 3, 0, 1)
NT = (((1,), (1,)), ((), ()))


def iota(shape, dim):
    return lax.broadcasted_iota(jnp.int32, shape, dim)


def third(value):
    return (value * 171) >> 9


def kernel(
    load_hbm,
    oper_hbm,
    prec_hbm,
    coup_ref,
    kinv_ref,
    map_ref,
    live_ref,
    ids_ref,
    mult_out,
    res_out,
    oper,
    prec,
    loads,
    resid,
    direc,
    outgo,
    income,
    permute,
    wide,
    pick,
    spread,
    values,
    bmsg,
    brecv,
    kown,
    kplane,
    ksel,
    csave,
    dots,
    step_rows,
    beta_rows,
    zed,
    qdir,
    lsend,
    lrecv,
    zsend,
    zrecv,
    csend,
    crecv,
    fsend,
    frecv,
    s1send,
    s1recv,
    s2send,
    s2recv,
    load_sem,
    oper_sem,
    face_send,
    face_recv,
    b_send,
    b_recv,
    fan_send,
    fan_recv,
):
    c = lax.axis_index("cluster")
    s = lax.axis_index("sub")
    x, z_lo = c // 2, c % 2
    y, z_hi, core = s // 8, (s // 2) % 4, s % 2
    z = z_hi * 2 + z_lo
    group = x * 4 + y
    plane = group * 2 + core
    column = z * 2 + core
    side = x // 2

    def at(px, py, pz, pcore):
        return (px * 2 + pz % 2, py * 8 + (pz // 2) * 2 + pcore)

    def plane_peer(q):
        return at(q // 8, (q // 2) % 4, z, q % 2)

    def z_peer(q):
        return at(x, y, q, core)

    def column_peer(q):
        return at(x, y, q // 2, q % 2)

    def group_peer(q):
        return at(q // 4, q % 4, z, core)

    neighbours = (
        ((c + 7) % 8, s),
        ((c + 1) % 8, s),
        (c, (s + 31) % 32),
        (c, (s + 1) % 32),
        (c, (s + 28) % 32),
        (c, (s + 4) % 32),
    )

    barrier = pltpu.get_barrier_semaphore()
    for peer in neighbours:
        pl.semaphore_signal(barrier, inc=1, device_id=peer, device_id_type=MESH)

    def greet(peer_of, count, me):
        def body(k, carry):
            peer = peer_of(lax.rem(me + k, count))
            pl.semaphore_signal(barrier, inc=1, device_id=peer, device_id_type=MESH)
            return carry

        lax.fori_loop(1, count, body, 0)

    greet(plane_peer, 32, plane)
    greet(column_peer, 16, column)

    load_copies = []
    for face in range(6):
        copy = pltpu.make_async_copy(
            load_hbm.at[:, pl.ds(face * FACE, FACE)], loads.at[face], load_sem.at[face]
        )
        copy.start()
        load_copies.append(copy)
    prec_copy = pltpu.make_async_copy(prec_hbm, prec, oper_sem.at[0])
    oper_copy = pltpu.make_async_copy(oper_hbm, oper, oper_sem.at[1])
    prec_copy.start()
    oper_copy.start()

    def rows_of(half):
        return pl.ds(pl.multiple_of(half * PART, PART), PART)

    def face_copy(turn, half, face):
        rows = rows_of(half)
        return pltpu.make_async_remote_copy(
            src_ref=loads.at[face, rows] if turn == 0 else outgo.at[turn - 1, face, rows],
            dst_ref=income.at[turn, face ^ 1, rows],
            send_sem=face_send.at[turn, half, face],
            recv_sem=face_recv.at[turn, half, face ^ 1],
            device_id=neighbours[face],
            device_id_type=MESH,
        )

    def face_wait(sem, turn, half, face):
        part = income.at[turn, face, rows_of(half)]
        pltpu.make_async_copy(part, part, sem.at[turn, half, face]).wait()

    def fan_out(slot, peer_of, count, me, source_of, dest):
        def body(k, carry):
            q = lax.rem(me + k, count)
            pltpu.make_async_remote_copy(
                src_ref=source_of(q),
                dst_ref=dest.at[me],
                send_sem=fan_send.at[slot],
                recv_sem=fan_recv.at[slot],
                device_id=peer_of(q),
                device_id_type=MESH,
            ).start()
            return carry

        lax.fori_loop(1, count, body, 0)

    def fan_wait(sem, slot, dest):
        part = dest.at[pl.ds(0, dest.shape[0] - 1)]
        pltpu.make_async_copy(part, part, sem.at[slot]).wait()

    pl.semaphore_wait(barrier, 6 + 31 + 15)

    for face in SEND_ORDER:
        load_copies[face].wait()
        face_copy(0, 0, face).start()

    turned = coup_ref[...].astype(F32)
    zero = jnp.zeros((8, FACE), F32)
    corner = iota((8, 128), 0)
    natural = jnp.zeros((8, 128), jnp.int32)
    placed = jnp.zeros((8, 128), jnp.int32)
    for k in range(8):
        number = jnp.full((8, 128), ids_ref[0, k], jnp.int32)
        nc, ns = number >> 5, number & 31
        nz = (((ns >> 1) & 3) << 1) + (nc & 1)
        np_ = ((nc >> 1) << 3) + ((ns >> 3) << 1) + (ns & 1)
        natural = jnp.where(corner == k, 3 * number, natural)
        placed = jnp.where(corner == k, nz * 128 + 3 * np_, placed)
    places = jnp.concatenate([natural, placed], axis=1).astype(F32)
    for face in range(6):
        bmsg[face, 0:24, :] = turned[:, face * FACE : (face + 1) * FACE]
        bmsg[face, 24:32, :] = places
    b_copies = []
    for face in SEND_ORDER:
        copy = pltpu.make_async_remote_copy(
            src_ref=bmsg.at[face],
            dst_ref=brecv.at[face ^ 1],
            send_sem=b_send.at[face],
            recv_sem=b_recv.at[face ^ 1],
            device_id=neighbours[face],
            device_id_type=MESH,
        )
        copy.start()
        b_copies.append(copy)
    for face in SEND_ORDER:
        face_copy(0, 1, face).start()

    kown[...] = jnp.zeros_like(kown)
    kown[0, 0:3, :] = kinv_ref[:, :HALF]
    kown[1, 0:3, :] = kinv_ref[:, HALF:]
    fan_out(0, plane_peer, 32, plane, lambda q: kown.at[q % 2], kplane)
    kplane[plane] = kown[core]

    def alive_of(face):
        return live_ref[0, face].astype(F32)

    def build_permute(face, carry):
        target = jnp.broadcast_to(map_ref[face], (FACE, FACE))
        hot = (iota((FACE, FACE), 0) == target).astype(F32)
        permute[face] = (hot * alive_of(face)).astype(BF16)
        return carry

    lax.fori_loop(0, 6, build_permute, 0)

    def clear(face, carry):
        for turn in range(4):
            outgo[turn, face] = jnp.zeros((ROWS, FACE), F32)
        return carry

    lax.fori_loop(0, 6, clear, 0)

    row = iota((32, 128), 0)
    which = third(row)
    part = (row - 3 * which).astype(F32)

    def one_hot(message):
        first = jnp.full((32, 128), -4.0, F32)
        second = jnp.full((32, 128), -4.0, F32)
        for k in range(8):
            line = message[24 + k : 25 + k, :]
            first = jnp.where(which == k, line[:, :128] + part, first)
            second = jnp.where(which == k, line[:, 128:] + part, second)
        load = jnp.concatenate([first] * 6, axis=1) == iota((32, 768), 1).astype(F32)
        field = jnp.concatenate([second] * 8, axis=1) == iota((32, 1024), 1).astype(F32)
        return load.astype(F32).astype(BF16), field.astype(F32).astype(BF16)

    def split(value):
        high = value.astype(BF16)
        low = (value - high.astype(F32)).astype(BF16)
        return jnp.concatenate([high, low], axis=0)

    def permuted(turn, face, rows):
        both = jnp.dot(
            split(income[turn, face, rows, :]), permute[face], preferred_element_type=F32
        )
        return both[:PART] + both[PART:]

    def fold(value):
        return value[:, :128] + value[:, 128:]

    def sweep(turn, half, update, matrix, products):
        rows = slice(half * PART, (half + 1) * PART)

        def body(face, carry):
            face_wait(face_recv, turn, half, face)
            value = update(face, rows)
            if matrix is not None:
                product = jnp.dot(
                    value.astype(BF16), matrix[face], preferred_element_type=F32
                )
                for n in range(6):
                    outgo[turn, n, rows, :] += product[:, n * FACE : (n + 1) * FACE]
            return carry

        if matrix is None:
            lax.fori_loop(0, 6, body, 0)
            return
        lax.fori_loop(0, 5, body, 0)
        face_wait(face_recv, turn, half, 5)
        rounded = update(5, rows).astype(BF16)
        totals = [jnp.zeros((PART, 128), F32)] * len(products)
        for n in SEND_ORDER:
            value = outgo[turn, n, rows, :] + jnp.dot(
                rounded, matrix[5, :, n * FACE : (n + 1) * FACE], preferred_element_type=F32
            )
            outgo[turn, n, rows, :] = value
            face_copy(turn + 1, half, n).start()
            totals = [
                total + fold(make(n, rows, value))
                for total, (_, make) in zip(totals, products)
            ]
        for total, (place, _) in zip(totals, products):
            dots[place, rows, :] = total

    def lane_row(place):
        return jnp.sum(dots[place].T, axis=0, keepdims=True)

    def spread_rows(line):
        wide_ = jnp.broadcast_to(line, (128, 128)).T
        return jnp.concatenate([wide_, wide_], axis=1)

    def scalars_start(slot, places):
        lines = [lane_row(place) for place in places]
        lines.append(jnp.zeros((4 - len(places), 128), F32))
        s1send[slot] = jnp.concatenate(lines, axis=0)
        fan_out(1 + slot, group_peer, 16, group, lambda q: s1send.at[slot], s1recv.at[slot])
        s1recv[slot, group] = s1send[slot]

    def scalars_middle(slot):
        fan_wait(fan_recv, 1 + slot, s1recv.at[slot])
        s2send[slot] = jnp.sum(s1recv[slot], axis=0)
        fan_out(5 + slot, column_peer, 16, column, lambda q: s2send.at[slot], s2recv.at[slot])
        s2recv[slot, column] = s2send[slot]

    def scalars_end(slot):
        fan_wait(fan_recv, 5 + slot, s2recv.at[slot])
        return jnp.sum(s2recv[slot], axis=0)

    def on_side(half, step, turn):
        @pl.when(side == half)
        def _():
            step(turn)

    def coarse_start(turn, half, source):
        rows = slice(half * PART, (half + 1) * PART)

        def body(face, terms):
            return terms + lax.dot_general(
                split(outgo[source, face, rows, :]), wide[face], NT, preferred_element_type=F32
            )

        terms = lax.fori_loop(0, 6, body, jnp.zeros((2 * PART, 256), F32))
        terms = terms[:PART] + terms[PART:]
        high = terms.astype(BF16)
        rest = terms - high.astype(F32)
        stacked = jnp.concatenate([high, split(rest)], axis=0)
        for part in range(2):
            full = jnp.dot(
                stacked,
                spread[:, part * HALF : (part + 1) * HALF],
                preferred_element_type=F32,
            )
            full = full[:PART] + full[PART : 2 * PART] + full[2 * PART :]
            lsend[turn, part, 8 * half : 8 * half + 8] = full.reshape(8, 8, HALF)

        def send(k, carry):
            q = 16 * half + lax.rem(plane + k, 16)

            @pl.when(q != plane)
            def _():
                pltpu.make_async_remote_copy(
                    src_ref=lsend.at[turn, q % 2, q // 2],
                    dst_ref=lrecv.at[turn, plane],
                    send_sem=fan_send.at[9 + turn],
                    recv_sem=fan_recv.at[9 + turn],
                    device_id=plane_peer(q),
                    device_id_type=MESH,
                ).start()

            return carry

        lax.fori_loop(0, 16, send, 0)

        @pl.when(side == half)
        def _():
            lrecv[turn, plane] = lsend[turn, core, group]

    def coarse_sum(turn):
        fan_wait(fan_recv, 9 + turn, lrecv.at[turn])
        zsend[turn] = jnp.sum(lrecv[turn], axis=0)
        fan_out(11 + turn, z_peer, 8, z, lambda q: zsend.at[turn], zrecv.at[turn])
        zrecv[turn, z] = zsend[turn]

    def coarse_apply(turn):
        fan_wait(fan_recv, 11 + turn, zrecv.at[turn])
        load = jnp.sum(zrecv[turn], axis=0)
        csend[turn] = lax.dot_general(
            load,
            ksel[...],
            NT,
            precision=lax.Precision.HIGHEST,
            preferred_element_type=F32,
        )
        fan_out(13 + turn, column_peer, 16, column, lambda q: csend.at[turn], crecv.at[turn])
        crecv[turn, column] = csend[turn]

    def coarse_share(turn):
        fan_wait(fan_recv, 13 + turn, crecv.at[turn])
        energy = jnp.zeros((8, 128), F32)
        cross = jnp.zeros((8, 128), F32)
        pieces = []
        for plane_z in range(8):
            both = crecv[turn, 2 * plane_z] + crecv[turn, 2 * plane_z + 1]
            field, load = both[:, :128], both[:, 128:]
            if turn == 0:
                csave[plane_z] = both
            else:
                saved = csave[plane_z]
                cross = cross + field * saved[:, 128:] + saved[:, :128] * load
            pieces.append(field)
            energy = energy + field * load
        lane = iota((8, 128), 1)
        energy = jnp.sum(energy, axis=1, keepdims=True)
        pieces[0] = jnp.where(lane == 96, energy, pieces[0])
        if turn == 1:
            cross = jnp.sum(cross, axis=1, keepdims=True)
            pieces[0] = jnp.where(lane == 97, cross, pieces[0])
        fsend[turn] = jnp.concatenate(pieces, axis=1)
        frecv[turn, group] = fsend[turn]

        def send(k, carry):
            q = lax.rem(group + k, 16)
            pltpu.make_async_remote_copy(
                src_ref=fsend.at[turn],
                dst_ref=frecv.at[turn, group],
                send_sem=fan_send.at[15 + turn],
                recv_sem=fan_recv.at[15 + turn + 2 * side],
                device_id=group_peer(q),
                device_id_type=MESH,
            ).start()
            return carry

        lax.fori_loop(1, 16, send, 0)

    def coarse_arrived(turn, half):
        def wait(count):
            part = frecv.at[turn, pl.ds(8 * half, count)]
            pltpu.make_async_copy(part, part, fan_recv.at[15 + turn + 2 * half]).wait()

        @pl.when(side == half)
        def _():
            wait(7)

        @pl.when(side != half)
        def _():
            wait(8)

    def coarse_values(turn, half):
        rows = slice(half * PART, (half + 1) * PART)
        field = frecv[turn, 8 * half : 8 * half + 8].reshape(PART, 1024)
        energy = field[:, 96:97]
        if turn == 1:
            before = frecv[0, 8 * half : 8 * half + 8].reshape(PART, 1024)
            beta = beta_rows[rows, :]
            energy = energy + beta[:, 0:1] * (
                field[:, 97:98] + beta[:, 0:1] * before[:, 96:97]
            )
            field = field + jnp.concatenate([beta] * 4, axis=1) * before
        values[rows, :] = lax.dot_general(
            field.astype(BF16), pick[...], NT, preferred_element_type=F32
        ).astype(BF16)
        return jnp.broadcast_to(energy, (PART, FACE))

    def first_residual(face, rows):
        value = alive_of(face) * loads[face, rows, :] + permuted(0, face, rows)
        resid[face, rows, :] = value
        return value

    def first_direction(face, rows):
        value = alive_of(face) * outgo[0, face, rows, :] + permuted(1, face, rows)
        direc[face, rows, :] = value
        return value

    def second_residual(face, rows):
        cols = pl.ds(pl.multiple_of(face * FACE, FACE), FACE)
        direct = alive_of(face) * outgo[1, face, rows, :] + permuted(2, face, rows)
        qdir[face, rows, :] = direct
        image = direct + jnp.dot(values[rows, :], wide[face], preferred_element_type=F32)
        step = step_rows[rows, :]
        mult_out[rows, cols] = step * direc[face, rows, :]
        value = resid[face, rows, :] - step * image
        resid[face, rows, :] = value
        return value

    def second_precond(face, rows):
        value = alive_of(face) * outgo[2, face, rows, :] + permuted(3, face, rows)
        zed[face, rows, :] = value
        return value

    def last_residual(face, rows):
        cols = pl.ds(pl.multiple_of(face * FACE, FACE), FACE)
        step, beta = step_rows[rows, :], beta_rows[rows, :]
        image = (
            alive_of(face) * outgo[3, face, rows, :]
            + permuted(4, face, rows)
            + beta * qdir[face, rows, :]
            + jnp.dot(values[rows, :], wide[face], preferred_element_type=F32)
        )
        mult_out[rows, cols] += step * (zed[face, rows, :] + beta * direc[face, rows, :])
        res_out[rows, cols] = resid[face, rows, :] - step * image

    with_residual = lambda n, rows, value: resid[n, rows, :] * value
    with_direction = lambda n, rows, value: direc[n, rows, :] * value
    with_precond = lambda n, rows, value: zed[n, rows, :] * value
    crossed = (
        lambda n, rows, value: zed[n, rows, :] * outgo[1, n, rows, :]
        + direc[n, rows, :] * value
    )

    dots[...] = jnp.zeros_like(dots)
    prec_copy.wait()
    sweep(0, 0, first_residual, prec, [(0, with_residual)])

    wide[...] = jnp.zeros_like(wide)
    spread[...] = jnp.zeros_like(spread)
    pick[...] = jnp.zeros_like(pick)
    for face in range(6):
        wide[face, 0:32, :] = jnp.where(
            iota((32, FACE), 0) < 24, bmsg[face] * alive_of(face), 0.0
        ).astype(BF16)
    spread[0:32, :], pick[0:32, :] = one_hot(bmsg[0])
    for face in range(6):
        b_copies[SEND_ORDER.index(face ^ 1)].wait_recv()
        start = 32 * (face + 1)
        rest = jnp.where(iota((32, FACE), 0) < 24, brecv[face], 0.0).astype(BF16)
        wide[face, start : start + 32, :] = jnp.dot(
            rest, permute[face], preferred_element_type=F32
        ).astype(BF16)
        spread[start : start + 32, :], pick[start : start + 32, :] = one_hot(brecv[face])

    fan_wait(fan_recv, 0, kplane)
    line = iota((128, 256), 0)
    packed = third(line)
    choose = jnp.where(
        line < 96, (iota((128, 256), 1) == packed * 8 + line - 3 * packed).astype(F32), 0.0
    )
    ksel[0:128, :] = jnp.dot(
        choose,
        kplane[...].reshape(256, HALF),
        precision=lax.Precision.HIGHEST,
        preferred_element_type=F32,
    )
    line = iota((128, HALF), 0)
    packed = third(line)
    owner = (
        ((packed >> 3) * 2 + z_lo) * 32 + ((packed >> 1) & 3) * 8 + z_hi * 2 + (packed & 1)
    )
    wanted = 3 * owner + line - 3 * packed
    ksel[128:256, :] = jnp.where(
        line < 96, (iota((128, HALF), 1) + HALF * core == wanted).astype(F32), 0.0
    )
    coarse_start(0, 0, 0)
    sweep(0, 1, first_residual, prec, [(0, with_residual)])
    coarse_start(0, 1, 0)
    oper_copy.wait()
    on_side(0, coarse_sum, 0)
    on_side(0, coarse_apply, 0)
    sweep(1, 0, first_direction, oper, [(1, with_direction)])
    scalars_start(0, (0, 1))
    on_side(1, coarse_sum, 0)
    on_side(0, coarse_share, 0)
    on_side(1, coarse_apply, 0)
    scalars_middle(0)
    sweep(1, 1, first_direction, oper, [(1, with_direction)])
    scalars_start(1, (0, 1))
    on_side(1, coarse_share, 0)

    saved = []
    for half in range(2):
        rows = slice(half * PART, (half + 1) * PART)
        totals = scalars_end(half)
        saved.append(totals)
        coarse_arrived(0, half)
        energy = coarse_values(0, half)
        step_rows[rows, :] = spread_rows(totals[0:1])[rows] / (
            spread_rows(totals[1:2])[rows] + energy
        )
        if half == 0:
            scalars_middle(1)
        sweep(2, half, second_residual, prec, [(2, with_residual)])
        coarse_start(1, half, 2)
    second = [(3, with_precond), (4, crossed)]
    on_side(0, coarse_sum, 1)
    on_side(0, coarse_apply, 1)
    sweep(3, 0, second_precond, oper, second)
    scalars_start(2, (2, 3, 4))
    on_side(1, coarse_sum, 1)
    on_side(0, coarse_share, 1)
    on_side(1, coarse_apply, 1)
    scalars_middle(2)
    sweep(3, 1, second_precond, oper, second)
    scalars_start(3, (2, 3, 4))
    on_side(1, coarse_share, 1)

    for half in range(2):
        rows = slice(half * PART, (half + 1) * PART)
        totals = scalars_end(2 + half)
        beta_line = totals[0:1] / saved[half][0:1]
        beta_rows[rows, :] = spread_rows(beta_line)[rows]
        curvature = totals[1:2] + beta_line * (totals[2:3] + beta_line * saved[half][1:2])
        coarse_arrived(1, half)
        energy = coarse_values(1, half)
        step_rows[rows, :] = spread_rows(totals[0:1])[rows] / (
            spread_rows(curvature)[rows] + energy
        )
        if half == 0:
            scalars_middle(3)
        sweep(4, half, last_residual, None, None)

    def drain(index, carry):
        half, face = index // 6, lax.rem(index, 6)
        for turn in range(5):
            face_wait(face_send, turn, half, face)
        return carry

    lax.fori_loop(0, 12, drain, 0)
    for copy in b_copies:
        copy.wait_send()
    fan_wait(fan_send, 0, kplane)
    for slot in range(4):
        fan_wait(fan_send, 1 + slot, s1recv.at[slot])
        fan_wait(fan_send, 5 + slot, s2recv.at[slot])
    for turn in range(2):
        fan_wait(fan_send, 9 + turn, lrecv.at[turn])
        fan_wait(fan_send, 11 + turn, zrecv.at[turn])
        fan_wait(fan_send, 13 + turn, crecv.at[turn])
        fan_wait(fan_send, 15 + turn, frecv.at[turn])


def local(load_terms, oper, prec, coupling, kinv, face_map, face_live, ids):
    any_ = pl.BlockSpec(memory_space=pl.ANY)
    vmem = pl.BlockSpec(memory_space=pltpu.VMEM)
    smem = pl.BlockSpec(memory_space=pltpu.SMEM)
    dma = pltpu.SemaphoreType.DMA

    def buf(*shape, dtype=F32):
        return pltpu.VMEM(shape, dtype)

    field = jax.ShapeDtypeStruct((ROWS, ORDER), F32)
    mult, res = pl.pallas_call(
        kernel,
        out_shape=(field, field),
        in_specs=[any_, any_, any_, vmem, vmem, vmem, smem, smem],
        out_specs=(vmem, vmem),
        scratch_shapes=[
            buf(6, FACE, ORDER, dtype=BF16),
            buf(6, FACE, ORDER, dtype=BF16),
            buf(6, ROWS, FACE),
            buf(6, ROWS, FACE),
            buf(6, ROWS, FACE),
            buf(4, 6, ROWS, FACE),
            buf(5, 6, ROWS, FACE),
            buf(6, FACE, FACE, dtype=BF16),
            buf(6, 256, FACE, dtype=BF16),
            buf(256, 1024, dtype=BF16),
            buf(256, 768, dtype=BF16),
            buf(ROWS, 256, dtype=BF16),
            buf(6, 32, FACE),
            buf(6, 32, FACE),
            buf(2, 8, HALF),
            buf(32, 8, HALF),
            buf(256, HALF),
            buf(8, 8, 256),
            buf(5, ROWS, 128),
            buf(ROWS, FACE),
            buf(ROWS, FACE),
            buf(6, ROWS, FACE),
            buf(6, ROWS, FACE),
            buf(2, 2, 16, 8, HALF),
            buf(2, 32, 8, HALF),
            buf(2, 8, HALF),
            buf(2, 8, 8, HALF),
            buf(2, 8, 256),
            buf(2, 16, 8, 256),
            buf(2, 8, 1024),
            buf(2, 16, 8, 1024),
            buf(4, 4, 128),
            buf(4, 16, 4, 128),
            buf(4, 4, 128),
            buf(4, 16, 4, 128),
            dma((6,)),
            dma((2,)),
            dma((5, 2, 6)),
            dma((5, 2, 6)),
            dma((6,)),
            dma((6,)),
            dma((19,)),
            dma((19,)),
        ],
        compiler_params=pltpu.CompilerParams(
            collective_id=0, has_side_effects=True, vmem_limit_bytes=60 * 1024 * 1024
        ),
        cost_estimate=pl.CostEstimate(
            flops=2_600_000_000, bytes_accessed=12_000_000, transcendentals=0
        ),
        name="feti_solve",
    )(
        load_terms[0],
        oper.reshape(6, FACE, ORDER),
        prec.reshape(6, FACE, ORDER),
        coupling[0].T,
        kinv,
        face_map.reshape(6, 1, FACE),
        face_live,
        ids,
    )
    return mult[None], res[None]


def solution(mesh):
    both = ("cluster", "sub")
    wide = P(both, None, None)
    flat = P(both, None)
    return jax.shard_map(
        local,
        mesh=mesh,
        in_specs=(wide, wide, wide, wide, flat, wide, flat, flat),
        out_specs=(wide, wide),
        check_vma=False,
    )
```
